32 devices in a mesh: groups: 2 (over x), adapt: 16 (over z, y, core).
Axes of the slice: x: 2, y: 2, z: 4, core: 2. Of those that a mesh axis runs over, the one named last changes fastest.
Arguments:
- activations: bfloat16 [4096, 12288], P(('groups', 'adapt')), parts along dimension 0, may hold values from -6 to 6
- cotangent: bfloat16 [4096, 512], P(('groups', 'adapt')), parts along dimension 0, may hold values from -6 to 6
- adapter_index_rows: int32 [4096], P(('groups', 'adapt')), parts along dimension 0, may hold values from 0 to 31, as said below
- frozen_weight: bfloat16 [12288, 512], P('adapt'), may hold values from -0.25 to 0.25
- adapter_down_weight: bfloat16 [32, 32, 12288], P('adapt'), may hold values from -0.0546875 to 0.0546875
- adapter_up_weight: bfloat16 [32, 32, 512], P('adapt'), may hold values from -0.25 to 0.25
Outputs:
- activation_gradient: bfloat16 [4096, 12288], P(('groups', 'adapt')), parts along dimension 0
- down_grad: bfloat16 [64, 32, 12288], P(('groups', 'adapt')), parts along dimension 0
- up_grad: bfloat16 [64, 32, 512], P(('groups', 'adapt')), parts along dimension 0
The draws below stay inside these ranges and needn't reach their ends.
There are 2 independent parts, one for each index of `groups`. The reference program is written for one: setup_inputs(seed, part) draws one part's arguments, and reference() takes and returns one part's arrays. A program takes and returns all parts, laid end to end along the dimension named above; an argument that names none is the same for every part. Nothing has to cross between parts.
Inputs may be any that keep to these rules, and one draw needn't show every extreme that they name: `adapter_index_rows`: adapters o * 2 to o * 2 + 1 are held by index o of adapt. Among the rows of one device each adapter appears at most 6 times, and the adapters of one owner at most 12 times together.
All inputs are finite; a program needn't handle non-finite values.
Results may differ from the reference program's by a relative error of at most 0.009.
Values may be sent and summed in bfloat16 or wider, within the bound.
No kernel may reach another device: no remote copies, remote signals or barrier semaphores. Data moves between devices by JAX's collectives and lax.ppermute only.
A program may use at most 192 MiB of HBM per device.

```python
import jax
import jax.numpy as jnp
from jax import lax

MODEL_WIDTH = 12288
OUTPUT_FEATURES = 512
ADAPTER_RANK = 32
ADP_DEV = 2
ADAPTER_COUNT = 32
ROWS_DEV = 128
ROWS = 2048
OWNER_MOST = 12
MOST = 6


def draw_adapter_index_rows(key, part):
    key = jax.random.fold_in(key, 11)
    owners = ADAPTER_COUNT // ADP_DEV
    blocks = ROWS // ROWS_DEV
    hot = jax.random.randint(jax.random.fold_in(key, 1), (), 0, ADAPTER_COUNT)
    levels = jax.random.randint(jax.random.fold_in(key, 2), (owners,), 0, 4)
    weights = levels * levels
    owner_of = jnp.repeat(jnp.arange(owners, dtype=jnp.int32), OWNER_MOST)
    place = jnp.tile(jnp.arange(OWNER_MOST, dtype=jnp.int32), owners)
    is_hot = (owner_of == hot // ADP_DEV).astype(jnp.int32)
    total = owners * OWNER_MOST

    def one_block(adapter_index):
        block_key = jax.random.fold_in(key, adapter_index + 100)
        shifts = jax.random.randint(jax.random.fold_in(block_key, 3), (owners,), 0, ADP_DEV)
        shift = jnp.where(is_hot == 1, hot % ADP_DEV, shifts[owner_of])
        adapter = owner_of * ADP_DEV + (place + shift) % ADP_DEV
        noise = jax.random.randint(jax.random.fold_in(block_key, 5), (total,), 0, 1024)
        score = ((is_hot * 100 + weights[owner_of]) * 1024 + noise) * total + jnp.arange(total, dtype=jnp.int32)
        unused, chosen = lax.top_k(score, ROWS_DEV)
        selected_rows = adapter[chosen]
        return jax.random.permutation(jax.random.fold_in(block_key, 7), selected_rows)
    return jax.vmap(one_block)(jnp.arange(blocks, dtype=jnp.int32)).reshape(ROWS).astype(jnp.int32)


def shard_levels(rng, dims, pieces, smallest, largest):
    def one(position, parts):
        draws = jax.random.uniform(jax.random.fold_in(jax.random.fold_in(rng, 6), position), (parts,), jnp.float32, smallest / len(pieces), largest / len(pieces))
        return jnp.repeat(jnp.exp(draws), dims[position] // parts).reshape((-1,) + (1,) * (len(dims) - position - 1))

    gain = one(*pieces[0])
    for cut in pieces[1:]:
        gain = gain * one(*cut)
    return gain


def scatter_about(own_key, shape, spread, limit, split=(), kind=jnp.bfloat16):
    array = jax.random.normal(own_key, shape, jnp.float32) * spread
    if len(split) > 0:
        array = shard_levels(own_key, shape, split, -0.22, 0.18) * array
    return jnp.clip(array, min=-limit, max=limit).astype(kind)


def setup_inputs(seed: int = 0, part: int = 0) -> dict:
    arg_keys = jax.random.split(jax.random.key(seed), 7)
    part_keys = jax.random.split(jax.random.fold_in(arg_keys[6], part), 7)
    return {
        "activations": scatter_about(part_keys[0], (ROWS, MODEL_WIDTH), 1.0, 6.0, ((0, 16),)),
        "cotangent": scatter_about(part_keys[1], (ROWS, OUTPUT_FEATURES), 1.0, 6.0, ((0, 16),)),
        "adapter_index_rows": draw_adapter_index_rows(jax.random.fold_in(jax.random.fold_in(arg_keys[6], part), 71), part),
        "frozen_weight": scatter_about(arg_keys[3], (MODEL_WIDTH, OUTPUT_FEATURES), OUTPUT_FEATURES ** -0.5, 0.25, ((0, 16),)),
        "adapter_down_weight": scatter_about(arg_keys[4], (ADAPTER_COUNT, ADAPTER_RANK, MODEL_WIDTH), MODEL_WIDTH ** -0.5, 0.0546875, ((0, 16),)),
        "adapter_up_weight": scatter_about(arg_keys[5], (ADAPTER_COUNT, ADAPTER_RANK, OUTPUT_FEATURES), OUTPUT_FEATURES ** -0.5, 0.25, ((0, 16),)),
    }


ADAPTER_SCALE = 2.0


def reference(activations, cotangent, adapter_index_rows, frozen_weight, adapter_down_weight, adapter_up_weight):
    frozen_contribution = jnp.dot(cotangent, frozen_weight.T, preferred_element_type=jnp.float32).astype(jnp.bfloat16)
    capacity = MOST * (ROWS // ROWS_DEV)
    order = jnp.argsort(adapter_index_rows, stable=True).astype(jnp.int32)
    member = adapter_index_rows[:, None] == jnp.arange(ADAPTER_COUNT, dtype=jnp.int32)[None, :]
    counts = jnp.sum(member.astype(jnp.int32), axis=0).astype(jnp.int32)
    starts = (jnp.cumsum(counts) - counts).astype(jnp.int32)
    padded_order = jnp.concatenate([order, jnp.full((capacity,), ROWS, jnp.int32)])

    def adapter_grouped(loop_state, adapter_index):
        start = starts[adapter_index].astype(jnp.int32)
        selected_rows = lax.dynamic_slice(padded_order, (start,), (capacity,))
        valid = jnp.arange(capacity, dtype=jnp.int32) < counts[adapter_index]
        selected_rows = jnp.where(valid, selected_rows, ROWS).astype(jnp.int32)
        input_rows = jnp.take(activations, selected_rows, axis=0, mode="fill", fill_value=0)
        output_gradient_rows = jnp.take(cotangent, selected_rows, axis=0, mode="fill", fill_value=0)
        down_matrix = adapter_down_weight[adapter_index]
        reduced_rank_value = jnp.dot(input_rows, down_matrix.T, preferred_element_type=jnp.float32).astype(jnp.bfloat16)
        gradient_list = jnp.dot(output_gradient_rows, adapter_up_weight[adapter_index].T, preferred_element_type=jnp.float32).astype(jnp.bfloat16)
        down_gradient = (ADAPTER_SCALE * jnp.dot(gradient_list.T, input_rows, preferred_element_type=jnp.float32)).astype(jnp.bfloat16)
        up_gradient = (ADAPTER_SCALE * jnp.dot(reduced_rank_value.T, output_gradient_rows, preferred_element_type=jnp.float32)).astype(jnp.bfloat16)
        adapter_row_values = (ADAPTER_SCALE * jnp.dot(gradient_list, down_matrix, preferred_element_type=jnp.float32)).astype(jnp.bfloat16)
        loop_state = loop_state.at[selected_rows].set(adapter_row_values, mode="drop")
        return loop_state, (down_gradient, up_gradient)

    initial_state = jnp.zeros((ROWS, MODEL_WIDTH), jnp.bfloat16)
    adapter_contribution, output_gradient = lax.scan(adapter_grouped, initial_state, jnp.arange(ADAPTER_COUNT, dtype=jnp.int32))
    activation_gradient = (frozen_contribution.astype(jnp.float32) + adapter_contribution.astype(jnp.float32)).astype(jnp.bfloat16)
    return activation_gradient, output_gradient[0], output_gradient[1]
```

```python
import jax
import jax.numpy as jnp
from jax import lax
from jax.sharding import PartitionSpec as P

ADAPTER_SCALE = 2.0
F32 = jnp.float32
BF16 = jnp.bfloat16


def dot(a, b, dims):
    return lax.dot_general(a, b, (dims, ((), ())), preferred_element_type=F32)


def on_device(x, cot, ids, frozen, down, up):
    n = lax.axis_size("adapt")
    half = n // 2
    rows, width = x.shape
    out_width = cot.shape[1]
    held, rank, _ = down.shape
    block = width // n
    halves = [list(range(half)), list(range(half, n))]
    swap = [(i, (i + half) % n) for i in range(n)]
    here = lax.axis_index("adapt")
    my_half = here // half

    def exchange(parts):
        return lax.all_to_all(
            parts, "adapt", split_axis=0, concat_axis=0, tiled=True, axis_index_groups=halves
        )

    def to_all(part):
        return exchange(jnp.broadcast_to(part[None], (half,) + part.shape))

    def swapped(part):
        return lax.ppermute(part, "adapt", swap)

    def by_width(array):
        count = array.shape[0]
        parts = array.reshape(count, 2, half, block).transpose(2, 0, 1, 3)
        return exchange(parts.reshape(half, count, 2 * block)).reshape(half * count, 2 * block)

    def from_width(array):
        count = array.shape[0] // half
        parts = exchange(array.reshape(half, count, 2 * block))
        return parts.reshape(half, count, 2, block).transpose(1, 2, 0, 3).reshape(count, width)

    up_flat = up.reshape(held * rank, out_width)
    both_up = jnp.concatenate([up_flat, swapped(up_flat)], axis=0)
    half_ids = to_all(ids.reshape(1, rows)).reshape(half * rows)
    half_cot = to_all(cot).reshape(half * rows, out_width)
    half_up = to_all(both_up).reshape(half, 2, held * rank, out_width)
    up_mine = half_up[:, 0].reshape(half * held * rank, out_width)
    up_other = half_up[:, 1].reshape(half * held * rank, out_width)
    x_block = by_width(x)
    down_mine = by_width(down.reshape(held * rank, width))
    down_other = swapped(down_mine)
    frozen_other = swapped(frozen)

    column_adapter = jnp.arange(half * held * rank, dtype=jnp.int32) // rank
    mine = half_ids[:, None] == (column_adapter + my_half * half * held)[None, :]
    other = half_ids[:, None] == (column_adapter + (1 - my_half) * half * held)[None, :]

    def chosen(product, mask):
        return jnp.where(mask, product, 0.0)

    grads_other = chosen(dot(half_cot, up_other, ((1,), (1,))), other).astype(BF16)
    grads_mine = chosen(dot(half_cot, up_mine, ((1,), (1,))), mine).astype(BF16)

    sent = (ADAPTER_SCALE * dot(grads_other, x_block, ((0,), (0,)))).astype(BF16)
    arrived = swapped(sent)
    kept = ADAPTER_SCALE * dot(grads_mine, x_block, ((0,), (0,)))
    down_grad = from_width((kept + arrived.astype(F32)).astype(BF16))

    lower = jnp.where(my_half == 0, frozen, frozen_other)
    upper = jnp.where(my_half == 0, frozen_other, frozen)
    base = dot(half_cot, jnp.concatenate([lower, upper], axis=0), ((1,), (1,)))
    lora = dot(grads_mine, down_mine, ((1,), (0,))) + dot(grads_other, down_other, ((1,), (0,)))
    activation_gradient = from_width((base + ADAPTER_SCALE * lora).astype(BF16))

    low = chosen(dot(x_block, down_mine, ((1,), (1,))), mine) + chosen(
        dot(x_block, down_other, ((1,), (1,))), other
    )
    low = low.reshape(half * rows, half * held, rank).sum(axis=1)
    low = exchange(low.reshape(half, rows, rank)).sum(axis=0).astype(BF16)
    low = to_all(low).reshape(half * rows, rank)
    pair = jnp.arange(held, dtype=jnp.int32) + here % half * held
    pair = jnp.concatenate([pair + my_half * half * held, pair + (1 - my_half) * half * held])
    spread = jnp.where(
        half_ids[:, None, None] == pair[None, :, None], low[:, None, :], jnp.zeros((), BF16)
    )
    up_part = ADAPTER_SCALE * dot(
        spread.reshape(half * rows, 2 * held * rank), half_cot, ((0,), (0,))
    )
    up_part = up_part.reshape(2, held * rank, out_width)
    up_grad = (up_part[0] + swapped(up_part[1])).astype(BF16)
    return (
        activation_gradient,
        down_grad.reshape(held, rank, width),
        up_grad.reshape(held, rank, out_width),
    )


def solution(mesh):
    return jax.shard_map(
        on_device,
        mesh=mesh,
        in_specs=(
            P(("groups", "adapt"), None),
            P(("groups", "adapt"), None),
            P(("groups", "adapt")),
            P("adapt", None),
            P("adapt", None, None),
            P("adapt", None, None),
        ),
        out_specs=(
            P(("groups", "adapt"), None),
            P(("groups", "adapt"), None, None),
            P(("groups", "adapt"), None, None),
        ),
        check_vma=False,
    )
```

```python
import jax
import jax.numpy as jnp
from jax import lax
from jax.experimental import pallas as pl
from jax.experimental.pallas import tpu as pltpu
from jax.sharding import PartitionSpec as P

ADAPTER_SCALE = 2.0
F32 = jnp.float32
BF16 = jnp.bfloat16
LANES = 128
VMEM_BYTES = 48 * 1024 * 1024


def dot(a, b, dims):
    return lax.dot_general(a, b, (dims, ((), ())), preferred_element_type=F32)


def after(value, *earlier):
    return lax.optimization_barrier((value,) + earlier)[0]


def in_xla(x, cot, ids, frozen, down, up):
    n = lax.axis_size("adapt")
    groups = lax.axis_size("groups")
    half = n // 2
    rows, width = x.shape
    out_width = cot.shape[1]
    held, rank, _ = down.shape
    own = held * rank
    block = width // n
    halves = [list(range(half)), list(range(half, n))]
    swap = [(i, (i + half) % n) for i in range(n)]
    here = lax.axis_index("adapt")
    group = lax.axis_index("groups")
    my_half = here // half

    def exchange(parts):
        return lax.all_to_all(
            parts, "adapt", split_axis=0, concat_axis=0, tiled=True, axis_index_groups=halves
        )

    def swapped(part):
        return lax.ppermute(part, "adapt", swap)

    def across_groups(part):
        arrived = [part]
        for step in range(1, groups):
            ring = [(g, (g + step) % groups) for g in range(groups)]
            arrived.append(lax.ppermute(part, "groups", ring))
        return [lax.select_n((group - p) % groups, *arrived) for p in range(groups)]

    def by_width(array):
        return array.reshape(array.shape[0], 2, half, block).transpose(1, 2, 0, 3)

    frozen_piece = lax.dynamic_slice_in_dim(
        frozen, group * (block // groups), block // groups, axis=0
    )
    down_piece = lax.dynamic_slice_in_dim(
        down.reshape(own, width), group * (own // groups), own // groups, axis=0
    )
    up_flat = up.reshape(own, out_width)

    up_other = swapped(up_flat)
    frozen_arrived = swapped(frozen_piece)
    down_send = by_width(down_piece)
    down_send = jnp.concatenate([down_send[0], down_send[1]], axis=2)
    down_near = exchange(down_send)

    x_send = by_width(x)
    up_pair = jnp.concatenate([up_flat, up_other], axis=0)
    up_rows = jnp.pad(up_pair, ((0, max(0, rows - 2 * own)), (0, 0)))
    id_rows = jnp.broadcast_to(ids.astype(BF16)[:, None], (rows, LANES))
    small = jnp.concatenate([cot, up_rows, id_rows], axis=1)
    first = jnp.concatenate(
        [x_send[0], jnp.broadcast_to(small[None], (half,) + small.shape)], axis=2
    )
    first = exchange(after(first, down_near))
    second = exchange(after(x_send[1], first))

    down_near_all = across_groups(down_near)
    down_far_all = across_groups(swapped(down_near))
    frozen_far = jnp.concatenate(across_groups(frozen_arrived), axis=0)

    def joined(pieces):
        return jnp.stack(pieces, axis=1).reshape(half * own, 2 * block)

    down_near_all = joined(down_near_all)
    down_far_all = joined(down_far_all)

    x_first = first[:, :, :block].reshape(half * rows, block)
    x_second = second.reshape(half * rows, block)
    half_cot = first[:, :, block : block + out_width].reshape(half * rows, out_width)
    up_got = first[:, :, block + out_width : block + 2 * out_width]
    half_ids = first[:, :, block + 2 * out_width].reshape(half * rows).astype(jnp.int32)
    up_near = up_got[:, :own].reshape(half * own, out_width)
    up_far = up_got[:, own : 2 * own].reshape(half * own, out_width)

    adapter = jnp.arange(half * own, dtype=jnp.int32) // rank
    near_ids = adapter + my_half * half * held
    far_ids = adapter + (1 - my_half) * half * held

    def grads_across(up_maps, adapters):
        return jnp.where(
            adapters[:, None] == half_ids[None, :], dot(up_maps, half_cot, ((1,), (1,))), 0.0
        ).astype(BF16)

    grads_far = grads_across(up_far, far_ids)
    grads_near = grads_across(up_near, near_ids)

    def down_part(grads, values):
        return ADAPTER_SCALE * dot(grads, values, ((1,), (0,)))

    far_first = swapped(down_part(grads_far, x_first).astype(BF16))
    far_second = swapped(down_part(grads_far, x_second).astype(BF16))
    sum_first = (down_part(grads_near, x_first) + far_first.astype(F32)).astype(BF16)
    sum_second = (down_part(grads_near, x_second) + far_second.astype(F32)).astype(BF16)

    low_frozen = jnp.where(my_half == 0, frozen, frozen_far)
    high_frozen = jnp.where(my_half == 0, frozen_far, frozen)
    base = dot(half_cot, jnp.concatenate([low_frozen, high_frozen], axis=0), ((1,), (1,)))
    lora = dot(grads_near, down_near_all, ((0,), (0,))) + dot(
        grads_far, down_far_all, ((0,), (0,))
    )
    gradient = (base + ADAPTER_SCALE * lora).astype(BF16).reshape(half, rows, 2 * block)

    x_block = jnp.concatenate([x_first, x_second], axis=1)
    fold = (
        jnp.arange(half * own, dtype=jnp.int32)[:, None] % rank
        == jnp.arange(LANES, dtype=jnp.int32)[None, :]
    ).astype(BF16)

    def low_part(maps, adapters):
        picked = jnp.where(
            half_ids[:, None] == adapters[None, :], dot(x_block, maps, ((1,), (1,))), 0.0
        ).astype(BF16)
        return dot(picked, fold, ((1,), (0,)))

    low = (low_part(down_near_all, near_ids) + low_part(down_far_all, far_ids)).astype(BF16)
    gradient = jnp.concatenate([gradient, low.reshape(half, rows, LANES)], axis=2)
    gradient = exchange(after(gradient, second))
    low = gradient[:, :, 2 * block : 2 * block + rank].astype(F32).sum(axis=0).astype(BF16)
    gradient = gradient[:, :, : 2 * block].reshape(half, rows, 2, block)
    gradient = gradient.transpose(1, 2, 0, 3).reshape(rows, width)

    pack = LANES // rank
    low_rows = low.reshape(pack, rows // pack, rank).transpose(1, 0, 2).reshape(rows // pack, LANES)
    low_rows = jnp.pad(low_rows, ((0, own - rows // pack), (0, 0)))
    sum_first = jnp.concatenate(
        [
            sum_first.reshape(half, own, block),
            jnp.broadcast_to(low_rows[None], (half, own, LANES)),
        ],
        axis=2,
    )
    sum_first = exchange(sum_first)
    sum_second = exchange(after(sum_second.reshape(half, own, block), sum_first))
    low = sum_first[:, : rows // pack, block:].reshape(half, rows // pack, pack, rank)
    low = low.transpose(0, 2, 1, 3).reshape(half * rows, rank)
    down_grad = jnp.stack([sum_first[:, :, :block], sum_second], axis=0)
    down_grad = down_grad.transpose(2, 0, 1, 3).reshape(held, rank, width)

    pair = jnp.arange(held, dtype=jnp.int32) + here % half * held
    pair = jnp.concatenate([pair + my_half * half * held, pair + (1 - my_half) * half * held])
    spread = jnp.where(
        half_ids[:, None] == jnp.repeat(pair, rank)[None, :],
        jnp.tile(low, (1, 2 * held)),
        jnp.zeros((), BF16),
    )
    up_part = (ADAPTER_SCALE * dot(spread, half_cot, ((0,), (0,)))).reshape(2, own, out_width)
    up_grad = (up_part[0] + swapped(up_part[1])).astype(BF16)
    return gradient, down_grad, up_grad.reshape(held, rank, out_width)


def shape(*dims, kind=BF16):
    return jax.ShapeDtypeStruct(dims, kind)


def with_kernels(x, cot, ids, frozen, down, up):
    n = lax.axis_size("adapt")
    half = n // 2
    rows, width = x.shape
    out_width = cot.shape[1]
    held, rank, _ = down.shape
    own = held * rank
    piece = own // 2
    block = width // n
    pair = 2 * block
    half_rows = half * rows
    halves = [list(range(half)), list(range(half, n))]
    here = lax.axis_index("adapt")
    group = lax.axis_index("groups")
    my_half = here // half
    core = here % 2

    def exchange(parts):
        return lax.all_to_all(
            parts, "adapt", split_axis=0, concat_axis=0, tiled=True, axis_index_groups=halves
        )

    def swapped(part):
        return lax.ppermute(part, "adapt", [(i, (i + half) % n) for i in range(n)])

    def flipped(part, bit):
        return lax.ppermute(part, "adapt", [(i, i ^ bit) for i in range(n)])

    def other_group(part):
        return lax.ppermute(part, "groups", [(0, 1), (1, 0)])

    smem = pl.BlockSpec(memory_space=pltpu.SMEM)
    vmem = pl.BlockSpec(memory_space=pltpu.VMEM)
    params = pltpu.CompilerParams(vmem_limit_bytes=VMEM_BYTES)

    def cost(flops, moved):
        return pl.CostEstimate(flops=flops, bytes_accessed=moved, transcendentals=0)

    frozen_piece = lax.dynamic_slice_in_dim(frozen, group * (block // 2), block // 2, axis=0)
    down_piece = lax.dynamic_slice_in_dim(down.reshape(own, width), group * piece, piece, axis=0)
    cot_at = pair
    up_at = cot_at + 2 * out_width
    id_at = up_at + out_width
    wide = id_at + LANES

    def pack_small(down_ref, cot_ref, up_ref, id_ref, out_ref):
        for j in range(half):
            c = j % 2
            for q in range(2):
                out_ref[j, :, q * block : (q + 1) * block] = down_ref[
                    :, (q * half + j) * block : (q * half + j + 1) * block
                ]
                out_ref[j, :, cot_at + q * out_width : cot_at + (q + 1) * out_width] = cot_ref[
                    (2 * c + q) * piece : (2 * c + q + 1) * piece, :
                ]
            out_ref[j, :, up_at:id_at] = up_ref[c * piece : (c + 1) * piece, :]
            out_ref[j, :, id_at:] = id_ref[...]

    id_line = jnp.broadcast_to(ids.astype(BF16)[None, :], (piece, LANES))
    small = pl.pallas_call(
        pack_small,
        out_shape=shape(half, piece, wide),
        compiler_params=params,
        cost_estimate=cost(0, 4 * half * piece * wide),
    )(down_piece, cot, up.reshape(own, out_width), id_line)
    small = exchange(small)

    def pack_rows(x_ref, out_ref):
        for j in range(half):
            for q in range(2):
                out_ref[j, :, q * block : (q + 1) * block] = x_ref[
                    :, (q * half + j) * block : (q * half + j + 1) * block
                ]

    x_parts = pl.pallas_call(
        pack_rows,
        out_shape=shape(half, rows, pair),
        compiler_params=params,
        cost_estimate=cost(0, 4 * rows * width),
    )(x)

    x_parts, small = lax.optimization_barrier((x_parts, small))
    x_block = exchange(x_parts).reshape(half_rows, pair)
    down_near = small[:, :, :pair].reshape(half * piece, pair)
    shared = small[:, :, pair:id_at].reshape(half * piece, 3 * out_width)
    frozen_near = swapped(after(frozen_piece, small))
    shared_far = swapped(shared[:, 2 * out_width :])
    shared_twin = flipped(shared, 1)
    down_far = swapped(down_near)
    near_cross = other_group(down_near)
    frozen_near, shared_far, shared_twin, down_far, near_cross = lax.optimization_barrier(
        (frozen_near, shared_far, shared_twin, down_far, near_cross)
    )
    up_far_twin = flipped(shared_far, 1)
    frozen_cross = other_group(frozen_near)
    far_cross = other_group(down_far)
    half_ids = small[:, 0, id_at:].reshape(half_rows).astype(F32)
    id_rows = jnp.broadcast_to(half_ids[:, None], (half_rows, LANES))
    id_lines = jnp.broadcast_to(half_ids[None, :], (8, half_rows))
    maps = (down_near, down_far, near_cross, far_cross)
    first_piece = jnp.where(group == 0, frozen_near, frozen_cross)
    last_piece = jnp.where(group == 0, frozen_cross, frozen_near)
    frozen_far = jnp.concatenate([first_piece, last_piece], axis=0)
    frozen_low = jnp.where(my_half == 0, frozen, frozen_far)
    frozen_high = jnp.where(my_half == 0, frozen_far, frozen)

    part = half * piece
    columns = 4 * part

    def column_ids(at, where, axis, dims):
        column = lax.broadcasted_iota(jnp.int32, dims, axis) + at
        crossed, rest = column // (2 * part), column % (2 * part)
        far, rest = rest // part, rest % part
        owner, within = rest // piece, rest % piece
        side = jnp.where(far == 0, where[0], 1 - where[0])
        which = jnp.where(crossed == 0, where[1], 1 - where[1])
        return ((side * half + owner) * held + (which * piece + within) // rank).astype(F32)

    where = jnp.stack([my_half, group, core])

    def grads_body(
        where_ref,
        mine_ref,
        twin_ref,
        far_ref,
        far_twin_ref,
        id_ref,
        line_ref,
        by_row_ref,
        by_column_ref,
        cot_ref,
        up_scratch,
    ):
        c = where_ref[2]
        for owner in range(half):
            at = owner * piece
            for q in range(2):
                for ref, side in ((mine_ref, c), (twin_ref, 1 - c)):
                    target = pl.multiple_of(owner * rows + (2 * side + q) * piece, piece)
                    cot_ref[pl.ds(target, piece), :] = ref[
                        at : at + piece, q * out_width : (q + 1) * out_width
                    ]
            for far, pieces in enumerate(
                (
                    (mine_ref[at : at + piece, 2 * out_width :], twin_ref[at : at + piece, 2 * out_width :]),
                    (far_ref[at : at + piece, :], far_twin_ref[at : at + piece, :]),
                )
            ):
                for side, value in zip((c, 1 - c), pieces):
                    crossed = jnp.where(side == where_ref[1], 0, 1)
                    target = (crossed * 2 + far) * part + at
                    up_scratch[pl.ds(pl.multiple_of(target, piece), piece), :] = value
        step = 2 * part
        for at in range(0, columns, step):
            product = dot(cot_ref[...], up_scratch[at : at + step, :], ((1,), (1,)))
            match = id_ref[:, :1] == column_ids(at, where_ref, 1, (1, step))
            by_row_ref[:, at : at + step] = jnp.where(match, product, 0.0).astype(BF16)
            product = dot(up_scratch[at : at + step, :], cot_ref[...], ((1,), (1,)))
            match = column_ids(at, where_ref, 0, (step, 1)) == line_ref[:1, :]
            by_column_ref[at : at + step, :] = jnp.where(match, product, 0.0).astype(BF16)

    by_row, by_column, half_cot = pl.pallas_call(
        grads_body,
        out_shape=(
            shape(half_rows, columns),
            shape(columns, half_rows),
            shape(half_rows, out_width),
        ),
        in_specs=[smem] + [vmem] * 6,
        out_specs=(vmem, vmem, vmem),
        scratch_shapes=[pltpu.VMEM((columns, out_width), BF16)],
        compiler_params=params,
        cost_estimate=cost(4 * half_rows * columns * out_width, 8 * half_rows * columns),
    )(where, shared, shared_twin, shared_far, up_far_twin, id_rows, id_lines)

    def down_part(far, values, kind):
        def body(grads_ref, x_ref, out_ref):
            out_ref[...] = (
                ADAPTER_SCALE * dot(grads_ref[...], x_ref[...], ((1,), (0,)))
            ).astype(kind)

        tile = pair // 3
        return pl.pallas_call(
            body,
            grid=(3, 2),
            out_shape=shape(2 * part, pair, kind=kind),
            in_specs=[
                pl.BlockSpec((part, half_rows), lambda c, p: (2 * p + far, 0)),
                pl.BlockSpec((half_rows, tile), lambda c, p: (0, c)),
            ],
            out_specs=pl.BlockSpec((part, tile), lambda c, p: (p, c)),
            compiler_params=params,
            cost_estimate=cost(4 * part * half_rows * pair, 2 * half_rows * pair),
        )(by_column, values)

    sent = down_part(1, x_block, BF16)
    arrived = swapped(sent)

    lines = 2 * rows

    def rows_body(cot_ref, grads_ref, low_w, high_w, m0, m1, m2, m3, out_ref):
        for q, w_ref in enumerate((low_w, high_w)):
            lo, hi = q * block, (q + 1) * block
            total = dot(cot_ref[...], w_ref[...], ((1,), (1,)))
            for s, m_ref in enumerate((m0, m1, m2, m3)):
                total = total + dot(
                    ADAPTER_SCALE * grads_ref[:, s * part : (s + 1) * part],
                    m_ref[:, lo:hi],
                    ((1,), (0,)),
                )
            out_ref[:, :, lo:hi] = total.astype(BF16).reshape(lines // rows, rows, block)

    cot_later = after(half_cot, sent)
    result = pl.pallas_call(
        rows_body,
        grid=(half_rows // lines,),
        out_shape=shape(half, rows, pair),
        in_specs=[
            pl.BlockSpec((lines, out_width), lambda i: (i, 0)),
            pl.BlockSpec((lines, columns), lambda i: (i, 0)),
        ]
        + [pl.BlockSpec((block, out_width), lambda i: (0, 0))] * 2
        + [pl.BlockSpec((part, pair), lambda i: (0, 0))] * 4,
        out_specs=pl.BlockSpec((lines // rows, rows, pair), lambda i: (i, 0, 0)),
        compiler_params=params,
        cost_estimate=cost(2 * half_rows * pair * (out_width + columns), 8 * half_rows * pair),
    )(cot_later, by_row, frozen_low, frozen_high, *maps)

    back = exchange(result)
    kept = down_part(0, after(x_block, result), F32)

    packed = LANES // rank

    def low_body(where_ref, x_ref, id_ref, m0, m1, m2, m3, out_ref):
        short = lines // packed
        low = jnp.zeros((short, LANES), F32)
        for s, m_ref in enumerate((m0, m1, m2, m3)):
            product = dot(x_ref[...], m_ref[...], ((1,), (1,)))
            match = id_ref[:, :1] == column_ids(s * part, where_ref, 1, (1, part))
            chosen = jnp.where(match, product, 0.0).astype(BF16)
            for t in range(packed):
                fold = (
                    lax.broadcasted_iota(jnp.int32, (part, LANES), 0) % rank + t * rank
                    == lax.broadcasted_iota(jnp.int32, (part, LANES), 1)
                ).astype(BF16)
                low = low + dot(chosen[t * short : (t + 1) * short, :], fold, ((1,), (0,)))
        out_ref[...] = low

    low = pl.pallas_call(
        low_body,
        grid=(half_rows // lines,),
        out_shape=shape(half_rows // packed, LANES, kind=F32),
        in_specs=[
            smem,
            pl.BlockSpec((lines, pair), lambda i: (i, 0)),
            pl.BlockSpec((lines, LANES), lambda i: (i, 0)),
        ]
        + [pl.BlockSpec((part, pair), lambda i: (0, 0))] * 4,
        out_specs=pl.BlockSpec((lines // packed, LANES), lambda i: (i, 0)),
        compiler_params=params,
        cost_estimate=cost(2 * half_rows * pair * columns, 2 * half_rows * pair),
    )(where, after(x_block, kept), id_rows, *maps)
    bit = 1
    while bit < half:
        low = low + flipped(low, bit)
        bit *= 2
    low = low.astype(BF16).reshape(half_rows // lines, lines // packed, packed, rank)
    low = low.transpose(0, 2, 1, 3).reshape(half_rows, rank)
    near = jnp.arange(held, dtype=jnp.int32) + here % half * held
    both = jnp.concatenate([near + my_half * half * held, near + (1 - my_half) * half * held])
    spread = jnp.where(
        half_ids[:, None] == jnp.repeat(both, rank)[None, :].astype(F32),
        jnp.tile(low, (1, 2 * held)),
        jnp.zeros((), BF16),
    )
    up_part = (ADAPTER_SCALE * dot(spread, half_cot, ((0,), (0,)))).reshape(2, own, out_width)


    arrived, up_part, kept = lax.optimization_barrier((arrived, up_part, kept))

    def add_body(kept_ref, arrived_ref, out_ref):
        for p in range(2):
            total = kept_ref[p * part : (p + 1) * part, :]
            total = total + arrived_ref[p * part : (p + 1) * part, :].astype(F32)
            out_ref[:, p * piece : (p + 1) * piece, :] = total.astype(BF16).reshape(
                half, piece, pair
            )

    sums = pl.pallas_call(
        add_body,
        out_shape=shape(half, own, pair),
        compiler_params=params,
        cost_estimate=cost(45000000000, 8 * half * own * pair),
    )(kept, arrived)
    home = exchange(after(sums, back))
    up_grad = (up_part[0] + swapped(after(up_part[1], sums))).astype(BF16)

    def unpack_rows(in_ref, out_ref):
        for j in range(half):
            for q in range(2):
                at = (q * half + j) * block
                out_ref[:, at : at + block] = in_ref[j, :, q * block : (q + 1) * block]

    gradient = pl.pallas_call(
        unpack_rows,
        out_shape=shape(rows, width),
        compiler_params=params,
        cost_estimate=cost(0, 4 * rows * width),
    )(back)

    def unpack_down(where_ref, in_ref, out_ref):
        for p in range(2):
            which = where_ref[1] if p == 0 else 1 - where_ref[1]
            target = pl.ds(pl.multiple_of(which * piece, piece), piece)
            for j in range(half):
                for q in range(2):
                    at = (q * half + j) * block
                    out_ref[target, at : at + block] = in_ref[
                        j, p * piece : (p + 1) * piece, q * block : (q + 1) * block
                    ]

    down_grad = pl.pallas_call(
        unpack_down,
        out_shape=shape(own, width),
        in_specs=[smem, vmem],
        out_specs=vmem,
        compiler_params=params,
        cost_estimate=cost(0, 4 * own * width),
    )(where, after(home, gradient))
    return gradient, down_grad.reshape(held, rank, width), up_grad.reshape(held, rank, out_width)


def on_device(x, cot, ids, frozen, down, up):
    n = lax.axis_size("adapt")
    own = down.shape[0] * down.shape[1]
    fits = (
        lax.axis_size("groups") == 2
        and x.shape[1] // n % (2 * LANES) == 0
        and down.shape[0] == 2
        and x.shape[0] == 2 * own == LANES
        and cot.shape[1] % LANES == 0
    )
    return (with_kernels if fits else in_xla)(x, cot, ids, frozen, down, up)


def solution(mesh):
    return jax.shard_map(
        on_device,
        mesh=mesh,
        in_specs=(
            P(("groups", "adapt"), None),
            P(("groups", "adapt"), None),
            P(("groups", "adapt")),
            P("adapt", None),
            P("adapt", None, None),
            P("adapt", None, None),
        ),
        out_specs=(
            P(("groups", "adapt"), None),
            P(("groups", "adapt"), None, None),
            P(("groups", "adapt"), None, None),
        ),
        check_vma=False,
    )
```

```python
import jax
import jax.numpy as jnp
from jax import lax
from jax.experimental import pallas as pl
from jax.experimental.pallas import tpu as pltpu
from jax.sharding import PartitionSpec as P

ADAPTER_SCALE = 2.0
F32 = jnp.float32
BF16 = jnp.bfloat16
LANES = 128
VMEM_BYTES = 48 * 1024 * 1024


def dot(a, b, dims):
    return lax.dot_general(a, b, (dims, ((), ())), preferred_element_type=F32)


def after(value, *earlier):
    return lax.optimization_barrier((value,) + earlier)[0]


def in_xla(x, cot, ids, frozen, down, up):
    n = lax.axis_size("adapt")
    groups = lax.axis_size("groups")
    half = n // 2
    rows, width = x.shape
    out_width = cot.shape[1]
    held, rank, _ = down.shape
    own = held * rank
    block = width // n
    halves = [list(range(half)), list(range(half, n))]
    swap = [(i, (i + half) % n) for i in range(n)]
    here = lax.axis_index("adapt")
    group = lax.axis_index("groups")
    my_half = here // half

    def exchange(parts):
        return lax.all_to_all(
            parts, "adapt", split_axis=0, concat_axis=0, tiled=True, axis_index_groups=halves
        )

    def swapped(part):
        return lax.ppermute(part, "adapt", swap)

    def across_groups(part):
        arrived = [part]
        for step in range(1, groups):
            ring = [(g, (g + step) % groups) for g in range(groups)]
            arrived.append(lax.ppermute(part, "groups", ring))
        return [lax.select_n((group - p) % groups, *arrived) for p in range(groups)]

    def by_width(array):
        return array.reshape(array.shape[0], 2, half, block).transpose(1, 2, 0, 3)

    frozen_piece = lax.dynamic_slice_in_dim(
        frozen, group * (block // groups), block // groups, axis=0
    )
    down_piece = lax.dynamic_slice_in_dim(
        down.reshape(own, width), group * (own // groups), own // groups, axis=0
    )
    up_flat = up.reshape(own, out_width)

    up_other = swapped(up_flat)
    frozen_arrived = swapped(frozen_piece)
    down_send = by_width(down_piece)
    down_send = jnp.concatenate([down_send[0], down_send[1]], axis=2)
    down_near = exchange(down_send)

    x_send = by_width(x)
    up_pair = jnp.concatenate([up_flat, up_other], axis=0)
    up_rows = jnp.pad(up_pair, ((0, max(0, rows - 2 * own)), (0, 0)))
    id_rows = jnp.broadcast_to(ids.astype(BF16)[:, None], (rows, LANES))
    small = jnp.concatenate([cot, up_rows, id_rows], axis=1)
    first = jnp.concatenate(
        [x_send[0], jnp.broadcast_to(small[None], (half,) + small.shape)], axis=2
    )
    first = exchange(after(first, down_near))
    second = exchange(after(x_send[1], first))

    down_near_all = across_groups(down_near)
    down_far_all = across_groups(swapped(down_near))
    frozen_far = jnp.concatenate(across_groups(frozen_arrived), axis=0)

    def joined(pieces):
        return jnp.stack(pieces, axis=1).reshape(half * own, 2 * block)

    down_near_all = joined(down_near_all)
    down_far_all = joined(down_far_all)

    x_first = first[:, :, :block].reshape(half * rows, block)
    x_second = second.reshape(half * rows, block)
    half_cot = first[:, :, block : block + out_width].reshape(half * rows, out_width)
    up_got = first[:, :, block + out_width : block + 2 * out_width]
    half_ids = first[:, :, block + 2 * out_width].reshape(half * rows).astype(jnp.int32)
    up_near = up_got[:, :own].reshape(half * own, out_width)
    up_far = up_got[:, own : 2 * own].reshape(half * own, out_width)

    adapter = jnp.arange(half * own, dtype=jnp.int32) // rank
    near_ids = adapter + my_half * half * held
    far_ids = adapter + (1 - my_half) * half * held

    def grads_across(up_maps, adapters):
        return jnp.where(
            adapters[:, None] == half_ids[None, :], dot(up_maps, half_cot, ((1,), (1,))), 0.0
        ).astype(BF16)

    grads_far = grads_across(up_far, far_ids)
    grads_near = grads_across(up_near, near_ids)

    def down_part(grads, values):
        return ADAPTER_SCALE * dot(grads, values, ((1,), (0,)))

    far_first = swapped(down_part(grads_far, x_first).astype(BF16))
    far_second = swapped(down_part(grads_far, x_second).astype(BF16))
    sum_first = (down_part(grads_near, x_first) + far_first.astype(F32)).astype(BF16)
    sum_second = (down_part(grads_near, x_second) + far_second.astype(F32)).astype(BF16)

    low_frozen = jnp.where(my_half == 0, frozen, frozen_far)
    high_frozen = jnp.where(my_half == 0, frozen_far, frozen)
    base = dot(half_cot, jnp.concatenate([low_frozen, high_frozen], axis=0), ((1,), (1,)))
    lora = dot(grads_near, down_near_all, ((0,), (0,))) + dot(
        grads_far, down_far_all, ((0,), (0,))
    )
    gradient = (base + ADAPTER_SCALE * lora).astype(BF16).reshape(half, rows, 2 * block)

    x_block = jnp.concatenate([x_first, x_second], axis=1)
    fold = (
        jnp.arange(half * own, dtype=jnp.int32)[:, None] % rank
        == jnp.arange(LANES, dtype=jnp.int32)[None, :]
    ).astype(BF16)

    def low_part(maps, adapters):
        picked = jnp.where(
            half_ids[:, None] == adapters[None, :], dot(x_block, maps, ((1,), (1,))), 0.0
        ).astype(BF16)
        return dot(picked, fold, ((1,), (0,)))

    low = (low_part(down_near_all, near_ids) + low_part(down_far_all, far_ids)).astype(BF16)
    gradient = jnp.concatenate([gradient, low.reshape(half, rows, LANES)], axis=2)
    gradient = exchange(after(gradient, second))
    low = gradient[:, :, 2 * block : 2 * block + rank].astype(F32).sum(axis=0).astype(BF16)
    gradient = gradient[:, :, : 2 * block].reshape(half, rows, 2, block)
    gradient = gradient.transpose(1, 2, 0, 3).reshape(rows, width)

    pack = LANES // rank
    low_rows = low.reshape(pack, rows // pack, rank).transpose(1, 0, 2).reshape(rows // pack, LANES)
    low_rows = jnp.pad(low_rows, ((0, own - rows // pack), (0, 0)))
    sum_first = jnp.concatenate(
        [
            sum_first.reshape(half, own, block),
            jnp.broadcast_to(low_rows[None], (half, own, LANES)),
        ],
        axis=2,
    )
    sum_first = exchange(sum_first)
    sum_second = exchange(after(sum_second.reshape(half, own, block), sum_first))
    low = sum_first[:, : rows // pack, block:].reshape(half, rows // pack, pack, rank)
    low = low.transpose(0, 2, 1, 3).reshape(half * rows, rank)
    down_grad = jnp.stack([sum_first[:, :, :block], sum_second], axis=0)
    down_grad = down_grad.transpose(2, 0, 1, 3).reshape(held, rank, width)

    pair = jnp.arange(held, dtype=jnp.int32) + here % half * held
    pair = jnp.concatenate([pair + my_half * half * held, pair + (1 - my_half) * half * held])
    spread = jnp.where(
        half_ids[:, None] == jnp.repeat(pair, rank)[None, :],
        jnp.tile(low, (1, 2 * held)),
        jnp.zeros((), BF16),
    )
    up_part = (ADAPTER_SCALE * dot(spread, half_cot, ((0,), (0,)))).reshape(2, own, out_width)
    up_grad = (up_part[0] + swapped(up_part[1])).astype(BF16)
    return gradient, down_grad, up_grad.reshape(held, rank, out_width)


def shape(*dims, kind=BF16):
    return jax.ShapeDtypeStruct(dims, kind)


def with_kernels(x, cot, ids, frozen, down, up):
    n = lax.axis_size("adapt")
    half = n // 2
    rows, width = x.shape
    out_width = cot.shape[1]
    held, rank, _ = down.shape
    own = held * rank
    piece = own // 2
    block = width // n
    pair = 2 * block
    half_rows = half * rows
    halves = [list(range(half)), list(range(half, n))]
    here = lax.axis_index("adapt")
    group = lax.axis_index("groups")
    my_half = here // half
    core = here % 2

    def exchange(parts):
        return lax.all_to_all(
            parts, "adapt", split_axis=0, concat_axis=0, tiled=True, axis_index_groups=halves
        )

    def swapped(part):
        return lax.ppermute(part, "adapt", [(i, (i + half) % n) for i in range(n)])

    def flipped(part, bit):
        return lax.ppermute(part, "adapt", [(i, i ^ bit) for i in range(n)])

    def other_group(part):
        return lax.ppermute(part, "groups", [(0, 1), (1, 0)])

    smem = pl.BlockSpec(memory_space=pltpu.SMEM)
    vmem = pl.BlockSpec(memory_space=pltpu.VMEM)
    params = pltpu.CompilerParams(vmem_limit_bytes=VMEM_BYTES)

    def cost(flops, moved):
        return pl.CostEstimate(flops=flops, bytes_accessed=moved, transcendentals=0)

    part = half * piece
    columns = 4 * part

    def column_ids(at, where, axis, dims):
        column = lax.broadcasted_iota(jnp.int32, dims, axis) + at
        crossed, rest = column // (2 * part), column % (2 * part)
        far, rest = rest // part, rest % part
        owner, within = rest // piece, rest % piece
        side = jnp.where(far == 0, where[0], 1 - where[0])
        which = jnp.where(crossed == 0, where[1], 1 - where[1])
        return ((side * half + owner) * held + (which * piece + within) // rank).astype(F32)


    where = jnp.stack([my_half, group, core])

    def grads_body(
        where_ref,
        mine_ref,
        twin_ref,
        id_ref,
        line_ref,
        by_row_ref,
        by_column_ref,
        cot_ref,
        up_scratch,
    ):
        c = where_ref[2]
        for owner in range(half):
            at = owner * piece
            for q in range(2):
                for ref, side in ((mine_ref, c), (twin_ref, 1 - c)):
                    target = pl.multiple_of(owner * rows + (2 * side + q) * piece, piece)
                    cot_ref[pl.ds(target, piece), :] = ref[
                        at : at + piece, q * out_width : (q + 1) * out_width
                    ]
            for far in range(2):
                lo, hi = (2 + far) * out_width, (3 + far) * out_width
                for ref, side in ((mine_ref, c), (twin_ref, 1 - c)):
                    crossed = jnp.where(side == where_ref[1], 0, 1)
                    target = (crossed * 2 + far) * part + at
                    up_scratch[pl.ds(pl.multiple_of(target, piece), piece), :] = ref[
                        at : at + piece, lo:hi
                    ]
        step = 2 * part
        for at in range(0, columns, step):
            product = dot(cot_ref[...], up_scratch[at : at + step, :], ((1,), (1,)))
            match = id_ref[:, :1] == column_ids(at, where_ref, 1, (1, step))
            by_row_ref[:, at : at + step] = jnp.where(match, product, 0.0).astype(BF16)
            product = dot(up_scratch[at : at + step, :], cot_ref[...], ((1,), (1,)))
            match = column_ids(at, where_ref, 0, (step, 1)) == line_ref[:1, :]
            by_column_ref[at : at + step, :] = jnp.where(match, product, 0.0).astype(BF16)

    low_frozen = jnp.where(my_half == 0, frozen, frozen_far)
    high_frozen = jnp.where(my_half == 0, frozen_far, frozen)
    base = dot(half_cot, jnp.concatenate([low_frozen, high_frozen], axis=0), ((1,), (1,)))
    lora = dot(grads_near, down_near_all, ((0,), (0,))) + dot(
        grads_far, down_far_all, ((0,), (0,))
    )
    gradient = (base + ADAPTER_SCALE * lora).astype(BF16).reshape(half, rows, 2 * block)

    x_block = jnp.concatenate([x_first, x_second], axis=1)
    fold = (
        jnp.arange(half * own, dtype=jnp.int32)[:, None] % rank
        == jnp.arange(LANES, dtype=jnp.int32)[None, :]
    ).astype(BF16)

    def low_part(maps, adapters):
        picked = jnp.where(
            half_ids[:, None] == adapters[None, :], dot(x_block, maps, ((1,), (1,))), 0.0
        ).astype(BF16)
        return dot(picked, fold, ((1,), (0,)))

    low = (low_part(down_near_all, near_ids) + low_part(down_far_all, far_ids)).astype(BF16)
    gradient = jnp.concatenate([gradient, low.reshape(half, rows, LANES)], axis=2)
    gradient = exchange(after(gradient, second))
    low = gradient[:, :, 2 * block : 2 * block + rank].astype(F32).sum(axis=0).astype(BF16)
    gradient = gradient[:, :, : 2 * block].reshape(half, rows, 2, block)
    gradient = gradient.transpose(1, 2, 0, 3).reshape(rows, width)

    pack = LANES // rank
    low_rows = low.reshape(pack, rows // pack, rank).transpose(1, 0, 2).reshape(rows // pack, LANES)
    low_rows = jnp.pad(low_rows, ((0, own - rows // pack), (0, 0)))
    sum_first = jnp.concatenate(
        [
            sum_first.reshape(half, own, block),
            jnp.broadcast_to(low_rows[None], (half, own, LANES)),
        ],
        axis=2,
    )
    sum_first = exchange(sum_first)
    sum_second = exchange(after(sum_second.reshape(half, own, block), sum_first))
    low = sum_first[:, : rows // pack, block:].reshape(half, rows // pack, pack, rank)
    low = low.transpose(0, 2, 1, 3).reshape(half * rows, rank)
    down_grad = jnp.stack([sum_first[:, :, :block], sum_second], axis=0)
    down_grad = down_grad.transpose(2, 0, 1, 3).reshape(held, rank, width)

    pair = jnp.arange(held, dtype=jnp.int32) + here % half * held
    pair = jnp.concatenate([pair + my_half * half * held, pair + (1 - my_half) * half * held])
    spread = jnp.where(
        half_ids[:, None] == jnp.repeat(pair, rank)[None, :],
        jnp.tile(low, (1, 2 * held)),
        jnp.zeros((), BF16),
    )
    up_part = (ADAPTER_SCALE * dot(spread, half_cot, ((0,), (0,)))).reshape(2, own, out_width)
    up_grad = (up_part[0] + swapped(up_part[1])).astype(BF16)
    return gradient, down_grad, up_grad.reshape(held, rank, out_width)


def shape(*dims, kind=BF16):
    return jax.ShapeDtypeStruct(dims, kind)


def with_kernels(x, cot, ids, frozen, down, up):
    n = lax.axis_size("adapt")
    half = n // 2
    rows, width = x.shape
    out_width = cot.shape[1]
    held, rank, _ = down.shape
    own = held * rank
    piece = own // 2
    block = width // n
    pair = 2 * block
    half_rows = half * rows
    halves = [list(range(half)), list(range(half, n))]
    here = lax.axis_index("adapt")
    group = lax.axis_index("groups")
    my_half = here // half
    core = here % 2

    def exchange(parts):
        return lax.all_to_all(
            parts, "adapt", split_axis=0, concat_axis=0, tiled=True, axis_index_groups=halves
        )

    def swapped(part):
        return lax.ppermute(part, "adapt", [(i, (i + half) % n) for i in range(n)])

    def flipped(part, bit):
        return lax.ppermute(part, "adapt", [(i, i ^ bit) for i in range(n)])

    def other_group(part):
        return lax.ppermute(part, "groups", [(0, 1), (1, 0)])

    smem = pl.BlockSpec(memory_space=pltpu.SMEM)
    vmem = pl.BlockSpec(memory_space=pltpu.VMEM)
    params = pltpu.CompilerParams(vmem_limit_bytes=VMEM_BYTES)

    def cost(flops, moved):
        return pl.CostEstimate(flops=flops, bytes_accessed=moved, transcendentals=0)

    frozen_piece = lax.dynamic_slice_in_dim(frozen, group * (block // 2), block // 2, axis=0)
    down_piece = lax.dynamic_slice_in_dim(down.reshape(own, width), group * piece, piece, axis=0)
    cot_at = pair
    up_at = cot_at + 2 * out_width
    id_at = up_at + 2 * out_width
    wide = id_at + LANES
    up_near = up.reshape(own, out_width)
    up_far = swapped(up_near)
    frozen_near = swapped(after(frozen_piece, up_far))

    def pack_small(down_ref, cot_ref, near_ref, far_ref, id_ref, out_ref):
        for j in range(half):
            c = j % 2
            for q in range(2):
                out_ref[j, :, q * block : (q + 1) * block] = down_ref[
                    :, (q * half + j) * block : (q * half + j + 1) * block
                ]
                out_ref[j, :, cot_at + q * out_width : cot_at + (q + 1) * out_width] = cot_ref[
                    (2 * c + q) * piece : (2 * c + q + 1) * piece, :
                ]
            for q, up_ref in enumerate((near_ref, far_ref)):
                out_ref[j, :, up_at + q * out_width : up_at + (q + 1) * out_width] = up_ref[
                    c * piece : (c + 1) * piece, :
                ]
            out_ref[j, :, id_at:] = id_ref[...]

    id_line = jnp.broadcast_to(ids.astype(BF16)[None, :], (piece, LANES))
    small = pl.pallas_call(
        pack_small,
        out_shape=shape(half, piece, wide),
        compiler_params=params,
        cost_estimate=cost(0, 4 * half * piece * wide),
    )(down_piece, cot, up_near, up_far, id_line)
    small = exchange(small)

    def pack_rows(x_ref, out_ref):
        for j in range(half):
            for q in range(2):
                out_ref[j, :, q * block : (q + 1) * block] = x_ref[
                    :, (q * half + j) * block : (q * half + j + 1) * block
                ]

    x_parts = pl.pallas_call(
        pack_rows,
        out_shape=shape(half, rows, pair),
        compiler_params=params,
        cost_estimate=cost(0, 4 * rows * width),
    )(x)

    x_parts, small, frozen_near = lax.optimization_barrier((x_parts, small, frozen_near))
    down_near = small[:, :, :pair].reshape(half * piece, pair)
    shared = small[:, :, pair:id_at].reshape(half * piece, 4 * out_width)
    shared_twin = flipped(shared, 1)
    x_block = exchange(after(x_parts, shared_twin)).reshape(half_rows, pair)
    down_far = swapped(down_near)
    near_cross = other_group(down_near)
    frozen_cross = other_group(frozen_near)
    half_ids = small[:, 0, id_at:].reshape(half_rows).astype(F32)
    id_rows = jnp.broadcast_to(half_ids[:, None], (half_rows, LANES))
    id_lines = jnp.broadcast_to(half_ids[None, :], (8, half_rows))
    first_piece = jnp.where(group == 0, frozen_near, frozen_cross)
    last_piece = jnp.where(group == 0, frozen_cross, frozen_near)
    frozen_far = jnp.concatenate([first_piece, last_piece], axis=0)
    frozen_low = jnp.where(my_half == 0, frozen, frozen_far)
    frozen_high = jnp.where(my_half == 0, frozen_far, frozen)

    part = half * piece
    columns = 4 * part

    def column_ids(at, where, axis, dims):
        column = lax.broadcasted_iota(jnp.int32, dims, axis) + at
        crossed, rest = column // (2 * part), column % (2 * part)
        far, rest = rest // part, rest % part
        owner, within = rest // piece, rest % piece
        side = jnp.where(far == 0, where[0], 1 - where[0])
        which = jnp.where(crossed == 0, where[1], 1 - where[1])
        return ((side * half + owner) * held + (which * piece + within) // rank).astype(F32)

    where = jnp.stack([my_half, group, core])

    def grads_body(
        where_ref,
        mine_ref,
        twin_ref,
        id_ref,
        line_ref,
        by_row_ref,
        by_column_ref,
        cot_ref,
        up_scratch,
    ):
        c = where_ref[2]
        for owner in range(half):
            at = owner * piece
            for q in range(2):
                for ref, side in ((mine_ref, c), (twin_ref, 1 - c)):
                    target = pl.multiple_of(owner * rows + (2 * side + q) * piece, piece)
                    cot_ref[pl.ds(target, piece), :] = ref[
                        at : at + piece, q * out_width : (q + 1) * out_width
                    ]
            for far in range(2):
                lo, hi = (2 + far) * out_width, (3 + far) * out_width
                for ref, side in ((mine_ref, c), (twin_ref, 1 - c)):
                    crossed = jnp.where(side == where_ref[1], 0, 1)
                    target = (crossed * 2 + far) * part + at
                    up_scratch[pl.ds(pl.multiple_of(target, piece), piece), :] = ref[
                        at : at + piece, lo:hi
                    ]
        step = 2 * part
        for at in range(0, columns, step):
            product = dot(cot_ref[...], up_scratch[at : at + step, :], ((1,), (1,)))
            match = id_ref[:, :1] == column_ids(at, where_ref, 1, (1, step))
            by_row_ref[:, at : at + step] = jnp.where(match, product, 0.0).astype(BF16)
            product = dot(up_scratch[at : at + step, :], cot_ref[...], ((1,), (1,)))
            match = column_ids(at, where_ref, 0, (step, 1)) == line_ref[:1, :]
            by_column_ref[at : at + step, :] = jnp.where(match, product, 0.0).astype(BF16)

    by_row, by_column, half_cot = pl.pallas_call(
        grads_body,
        out_shape=(
            shape(half_rows, columns),
            shape(columns, half_rows),
            shape(half_rows, out_width),
        ),
        in_specs=[smem] + [vmem] * 4,
        out_specs=(vmem, vmem, vmem),
        scratch_shapes=[pltpu.VMEM((columns, out_width), BF16)],
        compiler_params=params,
        cost_estimate=cost(4 * half_rows * columns * out_width, 8 * half_rows * columns),
    )(where, shared, shared_twin, id_rows, id_lines)

    far_cross = other_group(after(down_far, half_cot, frozen_low, frozen_high))
    maps = (down_near, down_far, near_cross, far_cross)

    lines = 2 * rows

    def rows_body(cot_ref, grads_ref, low_w, high_w, m0, m1, m2, m3, out_ref):
        for q, w_ref in enumerate((low_w, high_w)):
            lo, hi = q * block, (q + 1) * block
            total = dot(cot_ref[...], w_ref[...], ((1,), (1,)))
            for s, m_ref in enumerate((m0, m1, m2, m3)):
                total = total + dot(
                    ADAPTER_SCALE * grads_ref[:, s * part : (s + 1) * part],
                    m_ref[:, lo:hi],
                    ((1,), (0,)),
                )
            out_ref[:, :, lo:hi] = total.astype(BF16).reshape(lines // rows, rows, block)

    def down_part(far, values, kind):
        def body(first_ref, second_ref, x_ref, out_ref):
            for p, grads_ref in enumerate((first_ref, second_ref)):
                out_ref[p * part : (p + 1) * part, :] = (
                    ADAPTER_SCALE * dot(grads_ref[...], x_ref[...], ((1,), (0,)))
                ).astype(kind)

        tile = block // 2
        return pl.pallas_call(
            body,
            grid=(2,),
            out_shape=shape(2 * part, block, kind=kind),
            in_specs=[
                pl.BlockSpec((part, half_rows), lambda c: (far, 0)),
                pl.BlockSpec((part, half_rows), lambda c: (2 + far, 0)),
                pl.BlockSpec((half_rows, tile), lambda c: (0, c)),
            ],
            out_specs=pl.BlockSpec((2 * part, tile), lambda c: (0, c)),
            compiler_params=params,
            cost_estimate=cost(4 * part * half_rows * block, 2 * half_rows * block),
        )(by_column, by_column, values)

    packed = LANES // rank

    def low_body(where_ref, first_ref, second_ref, id_ref, m0, m1, m2, m3, out_ref):
        short = lines // packed
        low = jnp.zeros((short, LANES), F32)
        for s, m_ref in enumerate((m0, m1, m2, m3)):
            product = dot(first_ref[...], m_ref[:, :block], ((1,), (1,))) + dot(
                second_ref[...], m_ref[:, block:], ((1,), (1,))
            )
            match = id_ref[:, :1] == column_ids(s * part, where_ref, 1, (1, part))
            chosen = jnp.where(match, product, 0.0).astype(BF16)
            for t in range(packed):
                fold = (
                    lax.broadcasted_iota(jnp.int32, (part, LANES), 0) % rank + t * rank
                    == lax.broadcasted_iota(jnp.int32, (part, LANES), 1)
                ).astype(BF16)
                low = low + dot(chosen[t * short : (t + 1) * short, :], fold, ((1,), (0,)))
        out_ref[...] = low

    def add_body(first_ref, second_ref, kept_first_ref, kept_second_ref, out_ref):
        for q, (arrived_ref, kept_ref) in enumerate(
            ((first_ref, kept_first_ref), (second_ref, kept_second_ref))
        ):
            for p in range(2):
                total = kept_ref[p * part : (p + 1) * part, :]
                total = total + arrived_ref[p * part : (p + 1) * part, :].astype(F32)
                out_ref[:, p * piece : (p + 1) * piece, q * block : (q + 1) * block] = (
                    total.astype(BF16).reshape(half, piece, block)
                )

    def unpack_rows(in_ref, out_ref):
        for j in range(half):
            for q in range(2):
                at = (q * half + j) * block
                out_ref[:, at : at + block] = in_ref[j, :, q * block : (q + 1) * block]

    def unpack_down(where_ref, in_ref, out_ref):
        for p in range(2):
            which = where_ref[1] if p == 0 else 1 - where_ref[1]
            target = pl.ds(pl.multiple_of(which * piece, piece), piece)
            for j in range(half):
                for q in range(2):
                    at = (q * half + j) * block
                    out_ref[target, at : at + block] = in_ref[
                        j, p * piece : (p + 1) * piece, q * block : (q + 1) * block
                    ]


    frozen_piece = lax.dynamic_slice_in_dim(frozen, group * (block // 2), block // 2, axis=0)
    down_piece = lax.dynamic_slice_in_dim(down.reshape(own, width), group * piece, piece, axis=0)
    up_near = up.reshape(own, out_width)

    up_far = swapped(up_near)

    frozen_near = swapped(after(frozen_piece, up_far))

    cot_at = pair
    up_at = cot_at + 2 * out_width
    id_at = up_at + 2 * out_width
    wide = id_at + LANES

    def pack_small(down_ref, cot_ref, near_ref, far_ref, id_ref, out_ref):
        for j in range(half):
            c = j % 2
            for q in range(2):
                out_ref[j, :, q * block : (q + 1) * block] = down_ref[
                    :, (q * half + j) * block : (q * half + j + 1) * block
                ]
                out_ref[j, :, cot_at + q * out_width : cot_at + (q + 1) * out_width] = cot_ref[
                    (2 * c + q) * piece : (2 * c + q + 1) * piece, :
                ]
            for q, up_ref in enumerate((near_ref, far_ref)):
                out_ref[j, :, up_at + q * out_width : up_at + (q + 1) * out_width] = up_ref[
                    c * piece : (c + 1) * piece, :
                ]
            out_ref[j, :, id_at:] = id_ref[...]

    id_line = jnp.broadcast_to(ids.astype(BF16)[None, :], (piece, LANES))
    small = pl.pallas_call(
        pack_small,
        out_shape=shape(half, piece, wide),
        compiler_params=params,
        cost_estimate=cost(0, 4 * half * piece * wide),
    )(down_piece, cot, up_near, up_far, id_line)
    small = exchange(small)
    down_near = small[:, :, :pair].reshape(half * piece, pair)

    def pack_rows(x_ref, first_ref, second_ref):
        for j in range(half):
            for q, out_ref in enumerate((first_ref, second_ref)):
                out_ref[j, :, :] = x_ref[:, (q * half + j) * block : (q * half + j + 1) * block]

    x_parts = pl.pallas_call(
        pack_rows,
        out_shape=(shape(half, rows, block),) * 2,
        compiler_params=params,
        cost_estimate=cost(0, 4 * rows * width),
    )(x)

    small, frozen_near, x_parts = lax.optimization_barrier((small, frozen_near, x_parts))
    down_near = down_near if False else small[:, :, :pair].reshape(half * piece, pair)

    shared = small[:, :, pair:id_at].reshape(half * piece, 4 * out_width)
    half_ids = small[:, 0, id_at:].reshape(half_rows).astype(F32)
    id_rows = jnp.broadcast_to(half_ids[:, None], (half_rows, LANES))
    id_lines = jnp.broadcast_to(half_ids[None, :], (8, half_rows))

    shared_twin = flipped(shared, 1)

    down_far = swapped(down_near)

    near_cross = other_group(down_near)

    frozen_cross = other_group(frozen_near)

    first_piece = jnp.where(group == 0, frozen_near, frozen_cross)
    last_piece = jnp.where(group == 0, frozen_cross, frozen_near)
    frozen_far = jnp.concatenate([first_piece, last_piece], axis=0)
    frozen_low = jnp.where(my_half == 0, frozen, frozen_far)
    frozen_high = jnp.where(my_half == 0, frozen_far, frozen)

    x_first = exchange(after(x_parts[0], small, shared_twin)).reshape(half_rows, block)

    x_second = exchange(after(x_parts[1], x_first)).reshape(half_rows, block)

    by_row, by_column, half_cot = pl.pallas_call(
        grads_body,
        out_shape=(
            shape(half_rows, columns),
            shape(columns, half_rows),
            shape(half_rows, out_width),
        ),
        in_specs=[smem] + [vmem] * 4,
        out_specs=(vmem, vmem, vmem),
        scratch_shapes=[pltpu.VMEM((columns, out_width), BF16)],
        compiler_params=params,
        cost_estimate=cost(4 * half_rows * columns * out_width, 8 * half_rows * columns),
    )(where, shared, shared_twin, id_rows, id_lines)


    far_cross = other_group(after(down_far, half_cot, frozen_low, frozen_high))

    maps = (down_near, down_far, near_cross, far_cross)
    result = pl.pallas_call(
        rows_body,
        grid=(half_rows // lines,),
        out_shape=shape(half, rows, pair),
        in_specs=[
            pl.BlockSpec((lines, out_width), lambda i: (i, 0)),
            pl.BlockSpec((lines, columns), lambda i: (i, 0)),
        ]
        + [pl.BlockSpec((block, out_width), lambda i: (0, 0))] * 2
        + [pl.BlockSpec((part, pair), lambda i: (0, 0))] * 4,
        out_specs=pl.BlockSpec((lines // rows, rows, pair), lambda i: (i, 0, 0)),
        compiler_params=params,
        cost_estimate=cost(50000000000, 0),
    )(half_cot, by_row, frozen_low, frozen_high, *maps)


    back = exchange(result)

    sent_first = down_part(1, x_first, BF16)

    arrived_first = swapped(sent_first)

    sent_second = down_part(1, after(x_second, result, arrived_first), BF16)

    arrived_second = swapped(sent_second)

    low = pl.pallas_call(
        low_body,
        grid=(half_rows // lines,),
        out_shape=shape(half_rows // packed, LANES, kind=F32),
        in_specs=[
            smem,
            pl.BlockSpec((lines, block), lambda i: (i, 0)),
            pl.BlockSpec((lines, block), lambda i: (i, 0)),
            pl.BlockSpec((lines, LANES), lambda i: (i, 0)),
        ]
        + [pl.BlockSpec((part, pair), lambda i: (0, 0))] * 4,
        out_specs=pl.BlockSpec((lines // packed, LANES), lambda i: (i, 0)),
        compiler_params=params,
        cost_estimate=cost(2 * half_rows * pair * columns, 2 * half_rows * pair),
    )(where, x_first, after(x_second, sent_second), id_rows, *maps)

    kept_first = down_part(0, after(x_first, low), F32)
    kept_second = down_part(0, after(x_second, low), F32)

    low_sum = low
    for bit in (2, 1, 4):
        low_sum = low_sum + flipped(low_sum, bit)

    joined = lax.optimization_barrier((arrived_first, arrived_second, kept_first, kept_second, low_sum))
    sums = pl.pallas_call(
        add_body,
        out_shape=shape(half, own, pair),
        compiler_params=params,
        cost_estimate=cost(45000000000, 0),
    )(*joined[:4])

    home = exchange(after(sums, back))

    gradient = pl.pallas_call(
        unpack_rows,
        out_shape=shape(rows, width),
        compiler_params=params,
        cost_estimate=cost(0, 4 * rows * width),
    )(back)


    low_all = after(low_sum, sums, gradient)
    low_all = low_all.astype(BF16).reshape(half_rows // lines, lines // packed, packed, rank)
    low_all = low_all.transpose(0, 2, 1, 3).reshape(half_rows, rank)
    near = jnp.arange(held, dtype=jnp.int32) + here % half * held
    both = jnp.concatenate([near + my_half * half * held, near + (1 - my_half) * half * held])
    spread = jnp.where(
        half_ids[:, None] == jnp.repeat(both, rank)[None, :].astype(F32),
        jnp.tile(low_all, (1, 2 * held)),
        jnp.zeros((), BF16),
    )
    up_part = (ADAPTER_SCALE * dot(spread, half_cot, ((0,), (0,)))).reshape(2, own, out_width)

    up_grad = (up_part[0] + swapped(up_part[1])).astype(BF16)

    down_grad = pl.pallas_call(
        unpack_down,
        out_shape=shape(own, width),
        in_specs=[smem, vmem],
        out_specs=vmem,
        compiler_params=params,
        cost_estimate=cost(0, 4 * own * width),
    )(where, after(home, gradient))
    return gradient, down_grad.reshape(held, rank, width), up_grad.reshape(held, rank, out_width)


def on_device(x, cot, ids, frozen, down, up):
    n = lax.axis_size("adapt")
    own = down.shape[0] * down.shape[1]
    fits = (
        lax.axis_size("groups") == 2
        and x.shape[1] // n % (2 * LANES) == 0
        and n == 16
        and down.shape[0] == 2
        and x.shape[0] == 2 * own == LANES
        and cot.shape[1] % LANES == 0
    )
    return (with_kernels if fits else in_xla)(x, cot, ids, frozen, down, up)


def solution(mesh):
    return jax.shard_map(
        on_device,
        mesh=mesh,
        in_specs=(
            P(("groups", "adapt"), None),
            P(("groups", "adapt"), None),
            P(("groups", "adapt")),
            P("adapt", None),
            P("adapt", None, None),
            P("adapt", None, None),
        ),
        out_specs=(
            P(("groups", "adapt"), None),
            P(("groups", "adapt"), None, None),
            P(("groups", "adapt"), None, None),
        ),
        check_vma=False,
    )
```

```python
import jax
import jax.numpy as jnp
from jax import lax
from jax.experimental import pallas as pl
from jax.experimental.pallas import tpu as pltpu
from jax.sharding import PartitionSpec as P

ADAPTER_SCALE = 2.0
F32 = jnp.float32
BF16 = jnp.bfloat16
LANES = 128
VMEM_BYTES = 48 * 1024 * 1024


def dot(a, b, dims):
    return lax.dot_general(a, b, (dims, ((), ())), preferred_element_type=F32)


def after(value, *earlier):
    return lax.optimization_barrier((value,) + earlier)[0]


def in_xla(x, cot, ids, frozen, down, up):
    n = lax.axis_size("adapt")
    groups = lax.axis_size("groups")
    half = n // 2
    rows, width = x.shape
    out_width = cot.shape[1]
    held, rank, _ = down.shape
    own = held * rank
    block = width // n
    halves = [list(range(half)), list(range(half, n))]
    swap = [(i, (i + half) % n) for i in range(n)]
    here = lax.axis_index("adapt")
    group = lax.axis_index("groups")
    my_half = here // half

    def exchange(parts):
        return lax.all_to_all(
            parts, "adapt", split_axis=0, concat_axis=0, tiled=True, axis_index_groups=halves
        )

    def swapped(part):
        return lax.ppermute(part, "adapt", swap)

    def across_groups(part):
        arrived = [part]
        for step in range(1, groups):
            ring = [(g, (g + step) % groups) for g in range(groups)]
            arrived.append(lax.ppermute(part, "groups", ring))
        return [lax.select_n((group - p) % groups, *arrived) for p in range(groups)]

    def by_width(array):
        return array.reshape(array.shape[0], 2, half, block).transpose(1, 2, 0, 3)

    frozen_piece = lax.dynamic_slice_in_dim(
        frozen, group * (block // groups), block // groups, axis=0
    )
    down_piece = lax.dynamic_slice_in_dim(
        down.reshape(own, width), group * (own // groups), own // groups, axis=0
    )
    up_flat = up.reshape(own, out_width)

    up_other = swapped(up_flat)
    frozen_arrived = swapped(frozen_piece)
    down_send = by_width(down_piece)
    down_send = jnp.concatenate([down_send[0], down_send[1]], axis=2)
    down_near = exchange(down_send)

    x_send = by_width(x)
    up_pair = jnp.concatenate([up_flat, up_other], axis=0)
    up_rows = jnp.pad(up_pair, ((0, max(0, rows - 2 * own)), (0, 0)))
    id_rows = jnp.broadcast_to(ids.astype(BF16)[:, None], (rows, LANES))
    small = jnp.concatenate([cot, up_rows, id_rows], axis=1)
    first = jnp.concatenate(
        [x_send[0], jnp.broadcast_to(small[None], (half,) + small.shape)], axis=2
    )
    first = exchange(after(first, down_near))
    second = exchange(after(x_send[1], first))

    down_near_all = across_groups(down_near)
    down_far_all = across_groups(swapped(down_near))
    frozen_far = jnp.concatenate(across_groups(frozen_arrived), axis=0)

    def joined(pieces):
        return jnp.stack(pieces, axis=1).reshape(half * own, 2 * block)

    down_near_all = joined(down_near_all)
    down_far_all = joined(down_far_all)

    x_first = first[:, :, :block].reshape(half * rows, block)
    x_second = second.reshape(half * rows, block)
    half_cot = first[:, :, block : block + out_width].reshape(half * rows, out_width)
    up_got = first[:, :, block + out_width : block + 2 * out_width]
    half_ids = first[:, :, block + 2 * out_width].reshape(half * rows).astype(jnp.int32)
    up_near = up_got[:, :own].reshape(half * own, out_width)
    up_far = up_got[:, own : 2 * own].reshape(half * own, out_width)

    adapter = jnp.arange(half * own, dtype=jnp.int32) // rank
    near_ids = adapter + my_half * half * held
    far_ids = adapter + (1 - my_half) * half * held

    def grads_across(up_maps, adapters):
        return jnp.where(
            adapters[:, None] == half_ids[None, :], dot(up_maps, half_cot, ((1,), (1,))), 0.0
        ).astype(BF16)

    grads_far = grads_across(up_far, far_ids)
    grads_near = grads_across(up_near, near_ids)

    def down_part(grads, values):
        return ADAPTER_SCALE * dot(grads, values, ((1,), (0,)))

    far_first = swapped(down_part(grads_far, x_first).astype(BF16))
    far_second = swapped(down_part(grads_far, x_second).astype(BF16))
    sum_first = (down_part(grads_near, x_first) + far_first.astype(F32)).astype(BF16)
    sum_second = (down_part(grads_near, x_second) + far_second.astype(F32)).astype(BF16)

    low_frozen = jnp.where(my_half == 0, frozen, frozen_far)
    high_frozen = jnp.where(my_half == 0, frozen_far, frozen)
    base = dot(half_cot, jnp.concatenate([low_frozen, high_frozen], axis=0), ((1,), (1,)))
    lora = dot(grads_near, down_near_all, ((0,), (0,))) + dot(
        grads_far, down_far_all, ((0,), (0,))
    )
    gradient = (base + ADAPTER_SCALE * lora).astype(BF16).reshape(half, rows, 2 * block)

    x_block = jnp.concatenate([x_first, x_second], axis=1)
    fold = (
        jnp.arange(half * own, dtype=jnp.int32)[:, None] % rank
        == jnp.arange(LANES, dtype=jnp.int32)[None, :]
    ).astype(BF16)

    def low_part(maps, adapters):
        picked = jnp.where(
            half_ids[:, None] == adapters[None, :], dot(x_block, maps, ((1,), (1,))), 0.0
        ).astype(BF16)
        return dot(picked, fold, ((1,), (0,)))

    low = (low_part(down_near_all, near_ids) + low_part(down_far_all, far_ids)).astype(BF16)
    gradient = jnp.concatenate([gradient, low.reshape(half, rows, LANES)], axis=2)
    gradient = exchange(after(gradient, second))
    low = gradient[:, :, 2 * block : 2 * block + rank].astype(F32).sum(axis=0).astype(BF16)
    gradient = gradient[:, :, : 2 * block].reshape(half, rows, 2, block)
    gradient = gradient.transpose(1, 2, 0, 3).reshape(rows, width)

    pack = LANES // rank
    low_rows = low.reshape(pack, rows // pack, rank).transpose(1, 0, 2).reshape(rows // pack, LANES)
    low_rows = jnp.pad(low_rows, ((0, own - rows // pack), (0, 0)))
    sum_first = jnp.concatenate(
        [
            sum_first.reshape(half, own, block),
            jnp.broadcast_to(low_rows[None], (half, own, LANES)),
        ],
        axis=2,
    )
    sum_first = exchange(sum_first)
    sum_second = exchange(after(sum_second.reshape(half, own, block), sum_first))
    low = sum_first[:, : rows // pack, block:].reshape(half, rows // pack, pack, rank)
    low = low.transpose(0, 2, 1, 3).reshape(half * rows, rank)
    down_grad = jnp.stack([sum_first[:, :, :block], sum_second], axis=0)
    down_grad = down_grad.transpose(2, 0, 1, 3).reshape(held, rank, width)

    pair = jnp.arange(held, dtype=jnp.int32) + here % half * held
    pair = jnp.concatenate([pair + my_half * half * held, pair + (1 - my_half) * half * held])
    spread = jnp.where(
        half_ids[:, None] == jnp.repeat(pair, rank)[None, :],
        jnp.tile(low, (1, 2 * held)),
        jnp.zeros((), BF16),
    )
    up_part = (ADAPTER_SCALE * dot(spread, half_cot, ((0,), (0,)))).reshape(2, own, out_width)
    up_grad = (up_part[0] + swapped(up_part[1])).astype(BF16)
    return gradient, down_grad, up_grad.reshape(held, rank, out_width)


def shape(*dims, kind=BF16):
    return jax.ShapeDtypeStruct(dims, kind)


def with_kernels(x, cot, ids, frozen, down, up):
    n = lax.axis_size("adapt")
    half = n // 2
    rows, width = x.shape
    out_width = cot.shape[1]
    held, rank, _ = down.shape
    own = held * rank
    piece = own // 2
    block = width // n
    pair = 2 * block
    half_rows = half * rows
    halves = [list(range(half)), list(range(half, n))]
    here = lax.axis_index("adapt")
    group = lax.axis_index("groups")
    my_half = here // half
    core = here % 2

    def exchange(parts):
        return lax.all_to_all(
            parts, "adapt", split_axis=0, concat_axis=0, tiled=True, axis_index_groups=halves
        )

    def swapped(part):
        return lax.ppermute(part, "adapt", [(i, (i + half) % n) for i in range(n)])

    def flipped(part, bit):
        return lax.ppermute(part, "adapt", [(i, i ^ bit) for i in range(n)])

    def other_group(part):
        return lax.ppermute(part, "groups", [(0, 1), (1, 0)])

    smem = pl.BlockSpec(memory_space=pltpu.SMEM)
    vmem = pl.BlockSpec(memory_space=pltpu.VMEM)
    params = pltpu.CompilerParams(vmem_limit_bytes=VMEM_BYTES)

    def cost(flops, moved):
        return pl.CostEstimate(flops=flops, bytes_accessed=moved, transcendentals=0)

    part = half * piece
    columns = 4 * part

    def column_ids(at, where, axis, dims):
        column = lax.broadcasted_iota(jnp.int32, dims, axis) + at
        crossed, rest = column // (2 * part), column % (2 * part)
        far, rest = rest // part, rest % part
        owner, within = rest // piece, rest % piece
        side = jnp.where(far == 0, where[0], 1 - where[0])
        which = jnp.where(crossed == 0, where[1], 1 - where[1])
        return ((side * half + owner) * held + (which * piece + within) // rank).astype(F32)


    where = jnp.stack([my_half, group, core])

    def grads_body(
        where_ref,
        mine_ref,
        twin_ref,
        id_ref,
        line_ref,
        by_row_ref,
        by_column_ref,
        cot_ref,
        up_scratch,
    ):
        c = where_ref[2]
        for owner in range(half):
            at = owner * piece
            for q in range(2):
                for ref, side in ((mine_ref, c), (twin_ref, 1 - c)):
                    target = pl.multiple_of(owner * rows + (2 * side + q) * piece, piece)
                    cot_ref[pl.ds(target, piece), :] = ref[
                        at : at + piece, q * out_width : (q + 1) * out_width
                    ]
            for far in range(2):
                lo, hi = (2 + far) * out_width, (3 + far) * out_width
                for ref, side in ((mine_ref, c), (twin_ref, 1 - c)):
                    crossed = jnp.where(side == where_ref[1], 0, 1)
                    target = (crossed * 2 + far) * part + at
                    up_scratch[pl.ds(pl.multiple_of(target, piece), piece), :] = ref[
                        at : at + piece, lo:hi
                    ]
        step = 2 * part
        for at in range(0, columns, step):
            product = dot(cot_ref[...], up_scratch[at : at + step, :], ((1,), (1,)))
            match = id_ref[:, :1] == column_ids(at, where_ref, 1, (1, step))
            by_row_ref[:, at : at + step] = jnp.where(match, product, 0.0).astype(BF16)
            product = dot(up_scratch[at : at + step, :], cot_ref[...], ((1,), (1,)))
            match = column_ids(at, where_ref, 0, (step, 1)) == line_ref[:1, :]
            by_column_ref[at : at + step, :] = jnp.where(match, product, 0.0).astype(BF16)

    lines = 2 * rows

    def rows_body(cot_ref, grads_ref, low_w, high_w, m0, m1, m2, m3, out_ref):
        for q, w_ref in enumerate((low_w, high_w)):
            lo, hi = q * block, (q + 1) * block
            total = dot(cot_ref[...], w_ref[...], ((1,), (1,)))
            for s, m_ref in enumerate((m0, m1, m2, m3)):
                total = total + dot(
                    ADAPTER_SCALE * grads_ref[:, s * part : (s + 1) * part],
                    m_ref[:, lo:hi],
                    ((1,), (0,)),
                )
            out_ref[:, :, lo:hi] = total.astype(BF16).reshape(lines // rows, rows, block)

    def down_part(far, values, kind):
        def body(first_ref, second_ref, x_ref, out_ref):
            for p, grads_ref in enumerate((first_ref, second_ref)):
                out_ref[p * part : (p + 1) * part, :] = (
                    ADAPTER_SCALE * dot(grads_ref[...], x_ref[...], ((1,), (0,)))
                ).astype(kind)

        tile = block // 2
        return pl.pallas_call(
            body,
            grid=(2,),
            out_shape=shape(2 * part, block, kind=kind),
            in_specs=[
                pl.BlockSpec((part, half_rows), lambda c: (far, 0)),
                pl.BlockSpec((part, half_rows), lambda c: (2 + far, 0)),
                pl.BlockSpec((half_rows, tile), lambda c: (0, c)),
            ],
            out_specs=pl.BlockSpec((2 * part, tile), lambda c: (0, c)),
            compiler_params=params,
            cost_estimate=cost(4 * part * half_rows * block, 2 * half_rows * block),
        )(by_column, by_column, values)

    packed = LANES // rank

    def low_body(where_ref, first_ref, second_ref, id_ref, m0, m1, m2, m3, out_ref):
        short = lines // packed
        low = jnp.zeros((short, LANES), F32)
        for s, m_ref in enumerate((m0, m1, m2, m3)):
            product = dot(first_ref[...], m_ref[:, :block], ((1,), (1,))) + dot(
                second_ref[...], m_ref[:, block:], ((1,), (1,))
            )
            match = id_ref[:, :1] == column_ids(s * part, where_ref, 1, (1, part))
            chosen = jnp.where(match, product, 0.0).astype(BF16)
            for t in range(packed):
                fold = (
                    lax.broadcasted_iota(jnp.int32, (part, LANES), 0) % rank + t * rank
                    == lax.broadcasted_iota(jnp.int32, (part, LANES), 1)
                ).astype(BF16)
                low = low + dot(chosen[t * short : (t + 1) * short, :], fold, ((1,), (0,)))
        out_ref[...] = low

    def add_body(first_ref, second_ref, kept_first_ref, kept_second_ref, out_ref):
        for q, (arrived_ref, kept_ref) in enumerate(
            ((first_ref, kept_first_ref), (second_ref, kept_second_ref))
        ):
            for p in range(2):
                total = kept_ref[p * part : (p + 1) * part, :]
                total = total + arrived_ref[p * part : (p + 1) * part, :].astype(F32)
                out_ref[:, p * piece : (p + 1) * piece, q * block : (q + 1) * block] = (
                    total.astype(BF16).reshape(half, piece, block)
                )

    def unpack_rows(in_ref, out_ref):
        for j in range(half):
            for q in range(2):
                at = (q * half + j) * block
                out_ref[:, at : at + block] = in_ref[j, :, q * block : (q + 1) * block]

    def unpack_down(where_ref, in_ref, out_ref):
        for p in range(2):
            which = where_ref[1] if p == 0 else 1 - where_ref[1]
            target = pl.ds(pl.multiple_of(which * piece, piece), piece)
            for j in range(half):
                for q in range(2):
                    at = (q * half + j) * block
                    out_ref[target, at : at + block] = in_ref[
                        j, p * piece : (p + 1) * piece, q * block : (q + 1) * block
                    ]


    frozen_piece = lax.dynamic_slice_in_dim(frozen, group * (block // 2), block // 2, axis=0)
    down_piece = lax.dynamic_slice_in_dim(down.reshape(own, width), group * piece, piece, axis=0)
    up_near = up.reshape(own, out_width)

    up_far = swapped(up_near)

    frozen_near = swapped(after(frozen_piece, up_far))

    cot_at = pair
    up_at = cot_at + 2 * out_width
    id_at = up_at + 2 * out_width
    wide = id_at + LANES

    def pack_small(down_ref, cot_ref, near_ref, far_ref, id_ref, out_ref):
        for j in range(half):
            c = j % 2
            for q in range(2):
                out_ref[j, :, q * block : (q + 1) * block] = down_ref[
                    :, (q * half + j) * block : (q * half + j + 1) * block
                ]
                out_ref[j, :, cot_at + q * out_width : cot_at + (q + 1) * out_width] = cot_ref[
                    (2 * c + q) * piece : (2 * c + q + 1) * piece, :
                ]
            for q, up_ref in enumerate((near_ref, far_ref)):
                out_ref[j, :, up_at + q * out_width : up_at + (q + 1) * out_width] = up_ref[
                    c * piece : (c + 1) * piece, :
                ]
            out_ref[j, :, id_at:] = id_ref[...]

    id_line = jnp.broadcast_to(ids.astype(BF16)[None, :], (piece, LANES))
    small = pl.pallas_call(
        pack_small,
        out_shape=shape(half, piece, wide),
        compiler_params=params,
        cost_estimate=cost(0, 4 * half * piece * wide),
    )(down_piece, cot, up_near, up_far, id_line)
    small = exchange(small)
    down_near = small[:, :, :pair].reshape(half * piece, pair)

    def pack_rows(x_ref, first_ref, second_ref):
        for j in range(half):
            for q, out_ref in enumerate((first_ref, second_ref)):
                out_ref[j, :, :] = x_ref[:, (q * half + j) * block : (q * half + j + 1) * block]

    x_parts = pl.pallas_call(
        pack_rows,
        out_shape=(shape(half, rows, block),) * 2,
        compiler_params=params,
        cost_estimate=cost(0, 4 * rows * width),
    )(x)

    small, frozen_near, x_parts = lax.optimization_barrier((small, frozen_near, x_parts))
    down_near = small[:, :, :pair].reshape(half * piece, pair)

    shared = small[:, :, pair:id_at].reshape(half * piece, 4 * out_width)
    half_ids = small[:, 0, id_at:].reshape(half_rows).astype(F32)
    id_rows = jnp.broadcast_to(half_ids[:, None], (half_rows, LANES))
    id_lines = jnp.broadcast_to(half_ids[None, :], (8, half_rows))

    shared_twin = flipped(shared, 1)

    down_far = swapped(down_near)

    near_cross = other_group(down_near)

    frozen_cross = other_group(frozen_near)

    first_piece = jnp.where(group == 0, frozen_near, frozen_cross)
    last_piece = jnp.where(group == 0, frozen_cross, frozen_near)
    frozen_far = jnp.concatenate([first_piece, last_piece], axis=0)
    frozen_low = jnp.where(my_half == 0, frozen, frozen_far)
    frozen_high = jnp.where(my_half == 0, frozen_far, frozen)

    x_first = exchange(after(x_parts[0], small)).reshape(half_rows, block)

    x_second = exchange(after(x_parts[1], x_first)).reshape(half_rows, block)

    by_row, by_column, half_cot = pl.pallas_call(
        grads_body,
        out_shape=(
            shape(half_rows, columns),
            shape(columns, half_rows),
            shape(half_rows, out_width),
        ),
        in_specs=[smem] + [vmem] * 4,
        out_specs=(vmem, vmem, vmem),
        scratch_shapes=[pltpu.VMEM((columns, out_width), BF16)],
        compiler_params=params,
        cost_estimate=cost(4 * half_rows * columns * out_width, 8 * half_rows * columns),
    )(where, shared, shared_twin, id_rows, id_lines)


    far_cross = other_group(after(down_far, half_cot, frozen_low, frozen_high, x_first))

    maps = (down_near, down_far, near_cross, far_cross)
    result = pl.pallas_call(
        rows_body,
        grid=(half_rows // lines,),
        out_shape=shape(half, rows, pair),
        in_specs=[
            pl.BlockSpec((lines, out_width), lambda i: (i, 0)),
            pl.BlockSpec((lines, columns), lambda i: (i, 0)),
        ]
        + [pl.BlockSpec((block, out_width), lambda i: (0, 0))] * 2
        + [pl.BlockSpec((part, pair), lambda i: (0, 0))] * 4,
        out_specs=pl.BlockSpec((lines // rows, rows, pair), lambda i: (i, 0, 0)),
        compiler_params=params,
        cost_estimate=cost(16000000000, 0),
    )(half_cot, by_row, frozen_low, frozen_high, *maps)


    back = exchange(result)

    sent_first = down_part(1, x_first, BF16)

    arrived_first = swapped(sent_first)

    sent_second = down_part(1, after(x_second, result, arrived_first), BF16)

    arrived_second = swapped(sent_second)

    low = pl.pallas_call(
        low_body,
        grid=(half_rows // lines,),
        out_shape=shape(half_rows // packed, LANES, kind=F32),
        in_specs=[
            smem,
            pl.BlockSpec((lines, block), lambda i: (i, 0)),
            pl.BlockSpec((lines, block), lambda i: (i, 0)),
            pl.BlockSpec((lines, LANES), lambda i: (i, 0)),
        ]
        + [pl.BlockSpec((part, pair), lambda i: (0, 0))] * 4,
        out_specs=pl.BlockSpec((lines // packed, LANES), lambda i: (i, 0)),
        compiler_params=params,
        cost_estimate=cost(2 * half_rows * pair * columns, 2 * half_rows * pair),
    )(where, x_first, after(x_second, sent_second), id_rows, *maps)

    kept_first = down_part(0, after(x_first, low), F32)
    kept_second = down_part(0, after(x_second, low), F32)

    low_sum = low
    for bit in (2, 1):
        low_sum = low_sum + flipped(low_sum, bit)

    joined = lax.optimization_barrier((arrived_first, arrived_second, kept_first, kept_second, low_sum))
    low_sum = joined[4]
    sums = pl.pallas_call(
        add_body,
        out_shape=shape(half, own, pair),
        compiler_params=params,
        cost_estimate=cost(45000000000, 0),
    )(*joined[:4])

    home = exchange(after(sums, back))

    gradient = pl.pallas_call(
        unpack_rows,
        out_shape=shape(rows, width),
        compiler_params=params,
        cost_estimate=cost(0, 4 * rows * width),
    )(back)


    low_all = after(low_sum, sums, gradient)
    low_all = low_all.astype(BF16).reshape(half_rows // lines, lines // packed, packed, rank)
    low_all = low_all.transpose(0, 2, 1, 3).reshape(half_rows, rank)
    plane = half // 2
    planes = n // plane
    level = jnp.bitwise_xor(here // plane, jnp.arange(planes, dtype=jnp.int32))
    adapters = ((level * plane + here % plane) * held)[:, None] + jnp.arange(held, dtype=jnp.int32)
    spread = jnp.where(
        half_ids[:, None] == jnp.repeat(adapters.reshape(-1), rank)[None, :].astype(F32),
        jnp.tile(low_all, (1, planes * held)),
        jnp.zeros((), BF16),
    )
    up_part = (ADAPTER_SCALE * dot(spread, half_cot, ((0,), (0,)))).reshape(planes, own, out_width)
    up_sent = up_part.astype(BF16)

    up_grad = up_part[0]
    for level in range(1, planes):
        up_grad = up_grad + flipped(up_sent[level], level * plane).astype(F32)
    up_grad = up_grad.astype(BF16)

    down_grad = pl.pallas_call(
        unpack_down,
        out_shape=shape(own, width),
        in_specs=[smem, vmem],
        out_specs=vmem,
        compiler_params=params,
        cost_estimate=cost(0, 4 * own * width),
    )(where, after(home, gradient))
    return gradient, down_grad.reshape(held, rank, width), up_grad.reshape(held, rank, out_width)


def on_device(x, cot, ids, frozen, down, up):
    n = lax.axis_size("adapt")
    own = down.shape[0] * down.shape[1]
    fits = (
        lax.axis_size("groups") == 2
        and x.shape[1] // n % (2 * LANES) == 0
        and n == 16
        and down.shape[0] == 2
        and x.shape[0] == 2 * own == LANES
        and cot.shape[1] % LANES == 0
    )
    return (with_kernels if fits else in_xla)(x, cot, ids, frozen, down, up)


def solution(mesh):
    return jax.shard_map(
        on_device,
        mesh=mesh,
        in_specs=(
            P(("groups", "adapt"), None),
            P(("groups", "adapt"), None),
            P(("groups", "adapt")),
            P("adapt", None),
            P("adapt", None, None),
            P("adapt", None, None),
        ),
        out_specs=(
            P(("groups", "adapt"), None),
            P(("groups", "adapt"), None, None),
            P(("groups", "adapt"), None, None),
        ),
        check_vma=False,
    )
```

```python
import jax
import jax.numpy as jnp
from jax import lax
from jax.experimental import pallas as pl
from jax.experimental.pallas import tpu as pltpu
from jax.sharding import PartitionSpec as P

ADAPTER_SCALE = 2.0
F32 = jnp.float32
BF16 = jnp.bfloat16
LANES = 128
VMEM_BYTES = 28 * 1024 * 1024


def dot(a, b, dims):
    return lax.dot_general(a, b, (dims, ((), ())), preferred_element_type=F32)


def after(value, *earlier):
    return lax.optimization_barrier((value,) + earlier)[0]


def in_xla(x, cot, ids, frozen, down, up):
    n = lax.axis_size("adapt")
    groups = lax.axis_size("groups")
    half = n // 2
    rows, width = x.shape
    out_width = cot.shape[1]
    held, rank, _ = down.shape
    own = held * rank
    block = width // n
    halves = [list(range(half)), list(range(half, n))]
    swap = [(i, (i + half) % n) for i in range(n)]
    here = lax.axis_index("adapt")
    group = lax.axis_index("groups")
    my_half = here // half

    def exchange(parts):
        return lax.all_to_all(
            parts, "adapt", split_axis=0, concat_axis=0, tiled=True, axis_index_groups=halves
        )

    def swapped(part):
        return lax.ppermute(part, "adapt", swap)

    def across_groups(part):
        arrived = [part]
        for step in range(1, groups):
            ring = [(g, (g + step) % groups) for g in range(groups)]
            arrived.append(lax.ppermute(part, "groups", ring))
        return [lax.select_n((group - p) % groups, *arrived) for p in range(groups)]

    def by_width(array):
        return array.reshape(array.shape[0], 2, half, block).transpose(1, 2, 0, 3)

    frozen_piece = lax.dynamic_slice_in_dim(
        frozen, group * (block // groups), block // groups, axis=0
    )
    down_piece = lax.dynamic_slice_in_dim(
        down.reshape(own, width), group * (own // groups), own // groups, axis=0
    )
    up_flat = up.reshape(own, out_width)

    up_other = swapped(up_flat)
    frozen_arrived = swapped(frozen_piece)
    down_send = by_width(down_piece)
    down_send = jnp.concatenate([down_send[0], down_send[1]], axis=2)
    down_near = exchange(down_send)

    x_send = by_width(x)
    up_pair = jnp.concatenate([up_flat, up_other], axis=0)
    up_rows = jnp.pad(up_pair, ((0, max(0, rows - 2 * own)), (0, 0)))
    id_rows = jnp.broadcast_to(ids.astype(BF16)[:, None], (rows, LANES))
    small = jnp.concatenate([cot, up_rows, id_rows], axis=1)
    first = jnp.concatenate(
        [x_send[0], jnp.broadcast_to(small[None], (half,) + small.shape)], axis=2
    )
    first = exchange(after(first, down_near))
    second = exchange(after(x_send[1], first))

    down_near_all = across_groups(down_near)
    down_far_all = across_groups(swapped(down_near))
    frozen_far = jnp.concatenate(across_groups(frozen_arrived), axis=0)

    def joined(pieces):
        return jnp.stack(pieces, axis=1).reshape(half * own, 2 * block)

    down_near_all = joined(down_near_all)
    down_far_all = joined(down_far_all)

    x_first = first[:, :, :block].reshape(half * rows, block)
    x_second = second.reshape(half * rows, block)
    half_cot = first[:, :, block : block + out_width].reshape(half * rows, out_width)
    up_got = first[:, :, block + out_width : block + 2 * out_width]
    half_ids = first[:, :, block + 2 * out_width].reshape(half * rows).astype(jnp.int32)
    up_near = up_got[:, :own].reshape(half * own, out_width)
    up_far = up_got[:, own : 2 * own].reshape(half * own, out_width)

    adapter = jnp.arange(half * own, dtype=jnp.int32) // rank
    near_ids = adapter + my_half * half * held
    far_ids = adapter + (1 - my_half) * half * held

    def grads_across(up_maps, adapters):
        return jnp.where(
            adapters[:, None] == half_ids[None, :], dot(up_maps, half_cot, ((1,), (1,))), 0.0
        ).astype(BF16)

    grads_far = grads_across(up_far, far_ids)
    grads_near = grads_across(up_near, near_ids)

    def down_part(grads, values):
        return ADAPTER_SCALE * dot(grads, values, ((1,), (0,)))

    far_first = swapped(down_part(grads_far, x_first).astype(BF16))
    far_second = swapped(down_part(grads_far, x_second).astype(BF16))
    sum_first = (down_part(grads_near, x_first) + far_first.astype(F32)).astype(BF16)
    sum_second = (down_part(grads_near, x_second) + far_second.astype(F32)).astype(BF16)

    low_frozen = jnp.where(my_half == 0, frozen, frozen_far)
    high_frozen = jnp.where(my_half == 0, frozen_far, frozen)
    base = dot(half_cot, jnp.concatenate([low_frozen, high_frozen], axis=0), ((1,), (1,)))
    lora = dot(grads_near, down_near_all, ((0,), (0,))) + dot(
        grads_far, down_far_all, ((0,), (0,))
    )
    gradient = (base + ADAPTER_SCALE * lora).astype(BF16).reshape(half, rows, 2 * block)

    x_block = jnp.concatenate([x_first, x_second], axis=1)
    fold = (
        jnp.arange(half * own, dtype=jnp.int32)[:, None] % rank
        == jnp.arange(LANES, dtype=jnp.int32)[None, :]
    ).astype(BF16)

    def low_part(maps, adapters):
        picked = jnp.where(
            half_ids[:, None] == adapters[None, :], dot(x_block, maps, ((1,), (1,))), 0.0
        ).astype(BF16)
        return dot(picked, fold, ((1,), (0,)))

    low = (low_part(down_near_all, near_ids) + low_part(down_far_all, far_ids)).astype(BF16)
    gradient = jnp.concatenate([gradient, low.reshape(half, rows, LANES)], axis=2)
    gradient = exchange(after(gradient, second))
    low = gradient[:, :, 2 * block : 2 * block + rank].astype(F32).sum(axis=0).astype(BF16)
    gradient = gradient[:, :, : 2 * block].reshape(half, rows, 2, block)
    gradient = gradient.transpose(1, 2, 0, 3).reshape(rows, width)

    pack = LANES // rank
    low_rows = low.reshape(pack, rows // pack, rank).transpose(1, 0, 2).reshape(rows // pack, LANES)
    low_rows = jnp.pad(low_rows, ((0, own - rows // pack), (0, 0)))
    sum_first = jnp.concatenate(
        [
            sum_first.reshape(half, own, block),
            jnp.broadcast_to(low_rows[None], (half, own, LANES)),
        ],
        axis=2,
    )
    sum_first = exchange(sum_first)
    sum_second = exchange(after(sum_second.reshape(half, own, block), sum_first))
    low = sum_first[:, : rows // pack, block:].reshape(half, rows // pack, pack, rank)
    low = low.transpose(0, 2, 1, 3).reshape(half * rows, rank)
    down_grad = jnp.stack([sum_first[:, :, :block], sum_second], axis=0)
    down_grad = down_grad.transpose(2, 0, 1, 3).reshape(held, rank, width)

    pair = jnp.arange(held, dtype=jnp.int32) + here % half * held
    pair = jnp.concatenate([pair + my_half * half * held, pair + (1 - my_half) * half * held])
    spread = jnp.where(
        half_ids[:, None] == jnp.repeat(pair, rank)[None, :],
        jnp.tile(low, (1, 2 * held)),
        jnp.zeros((), BF16),
    )
    up_part = (ADAPTER_SCALE * dot(spread, half_cot, ((0,), (0,)))).reshape(2, own, out_width)
    up_grad = (up_part[0] + swapped(up_part[1])).astype(BF16)
    return gradient, down_grad, up_grad.reshape(held, rank, out_width)


def shape(*dims, kind=BF16):
    return jax.ShapeDtypeStruct(dims, kind)


def with_kernels(x, cot, ids, frozen, down, up):
    n = lax.axis_size("adapt")
    half = n // 2
    rows, width = x.shape
    out_width = cot.shape[1]
    held, rank, _ = down.shape
    own = held * rank
    piece = own // 2
    block = width // n
    pair = 2 * block
    half_rows = half * rows
    halves = [list(range(half)), list(range(half, n))]
    here = lax.axis_index("adapt")
    group = lax.axis_index("groups")
    my_half = here // half
    core = here % 2

    def exchange(parts):
        return lax.all_to_all(
            parts, "adapt", split_axis=0, concat_axis=0, tiled=True, axis_index_groups=halves
        )

    def swapped(part):
        return lax.ppermute(part, "adapt", [(i, (i + half) % n) for i in range(n)])

    def flipped(part, bit):
        return lax.ppermute(part, "adapt", [(i, i ^ bit) for i in range(n)])

    def other_group(part):
        return lax.ppermute(part, "groups", [(0, 1), (1, 0)])

    smem = pl.BlockSpec(memory_space=pltpu.SMEM)
    vmem = pl.BlockSpec(memory_space=pltpu.VMEM)
    params = pltpu.CompilerParams(vmem_limit_bytes=VMEM_BYTES)

    def cost(flops, moved):
        return pl.CostEstimate(flops=flops, bytes_accessed=moved, transcendentals=0)

    part = half * piece
    columns = 4 * part

    def column_ids(at, where, axis, dims):
        column = lax.broadcasted_iota(jnp.int32, dims, axis) + at
        crossed, rest = column // (2 * part), column % (2 * part)
        far, rest = rest // part, rest % part
        owner, within = rest // piece, rest % piece
        side = jnp.where(far == 0, where[0], 1 - where[0])
        which = jnp.where(crossed == 0, where[1], 1 - where[1])
        return ((side * half + owner) * held + (which * piece + within) // rank).astype(F32)


    where = jnp.stack([my_half, group, core])

    def grads_body(
        where_ref,
        mine_ref,
        twin_ref,
        id_ref,
        line_ref,
        by_row_ref,
        by_column_ref,
        cot_ref,
        up_scratch,
    ):
        c = where_ref[2]
        for owner in range(half):
            at = owner * piece
            for q in range(2):
                for ref, side in ((mine_ref, c), (twin_ref, 1 - c)):
                    target = pl.multiple_of(owner * rows + (2 * side + q) * piece, piece)
                    cot_ref[pl.ds(target, piece), :] = ref[
                        at : at + piece, q * out_width : (q + 1) * out_width
                    ]
            for far in range(2):
                lo, hi = (2 + far) * out_width, (3 + far) * out_width
                for ref, side in ((mine_ref, c), (twin_ref, 1 - c)):
                    crossed = jnp.where(side == where_ref[1], 0, 1)
                    target = (crossed * 2 + far) * part + at
                    up_scratch[pl.ds(pl.multiple_of(target, piece), piece), :] = ref[
                        at : at + piece, lo:hi
                    ]
        step = 2 * part
        for at in range(0, columns, step):
            product = dot(cot_ref[...], up_scratch[at : at + step, :], ((1,), (1,)))
            match = id_ref[:, :1] == column_ids(at, where_ref, 1, (1, step))
            by_row_ref[:, at : at + step] = jnp.where(match, product, 0.0).astype(BF16)
            product = dot(up_scratch[at : at + step, :], cot_ref[...], ((1,), (1,)))
            match = column_ids(at, where_ref, 0, (step, 1)) == line_ref[:1, :]
            by_column_ref[at : at + step, :] = jnp.where(match, product, 0.0).astype(BF16)

    lines = 2 * rows

    def rows_body(cot_ref, grads_ref, low_w, high_w, m0, m1, m2, m3, out_ref):
        for q, w_ref in enumerate((low_w, high_w)):
            lo, hi = q * block, (q + 1) * block
            total = dot(cot_ref[...], w_ref[...], ((1,), (1,)))
            for s, m_ref in enumerate((m0, m1, m2, m3)):
                total = total + dot(
                    ADAPTER_SCALE * grads_ref[:, s * part : (s + 1) * part],
                    m_ref[:, lo:hi],
                    ((1,), (0,)),
                )
            out_ref[:, :, lo:hi] = total.astype(BF16).reshape(lines // rows, rows, block)

    def down_part(far, values, kind):
        def body(first_ref, second_ref, x_ref, out_ref):
            for p, grads_ref in enumerate((first_ref, second_ref)):
                out_ref[p * part : (p + 1) * part, :] = (
                    ADAPTER_SCALE * dot(grads_ref[...], x_ref[...], ((1,), (0,)))
                ).astype(kind)

        tile = block // 2
        return pl.pallas_call(
            body,
            grid=(2,),
            out_shape=shape(2 * part, block, kind=kind),
            in_specs=[
                pl.BlockSpec((part, half_rows), lambda c: (far, 0)),
                pl.BlockSpec((part, half_rows), lambda c: (2 + far, 0)),
                pl.BlockSpec((half_rows, tile), lambda c: (0, c)),
            ],
            out_specs=pl.BlockSpec((2 * part, tile), lambda c: (0, c)),
            compiler_params=params,
            cost_estimate=cost(4 * part * half_rows * block, 2 * half_rows * block),
        )(by_column, by_column, values)

    packed = LANES // rank

    def low_body(where_ref, first_ref, second_ref, id_ref, m0, m1, m2, m3, out_ref):
        short = lines // packed
        low = jnp.zeros((short, LANES), F32)
        for s, m_ref in enumerate((m0, m1, m2, m3)):
            product = dot(first_ref[...], m_ref[:, :block], ((1,), (1,))) + dot(
                second_ref[...], m_ref[:, block:], ((1,), (1,))
            )
            match = id_ref[:, :1] == column_ids(s * part, where_ref, 1, (1, part))
            chosen = jnp.where(match, product, 0.0).astype(BF16)
            for t in range(packed):
                fold = (
                    lax.broadcasted_iota(jnp.int32, (part, LANES), 0) % rank + t * rank
                    == lax.broadcasted_iota(jnp.int32, (part, LANES), 1)
                ).astype(BF16)
                low = low + dot(chosen[t * short : (t + 1) * short, :], fold, ((1,), (0,)))
        out_ref[...] = low

    def add_body(first_ref, second_ref, kept_first_ref, kept_second_ref, out_ref):
        for q, (arrived_ref, kept_ref) in enumerate(
            ((first_ref, kept_first_ref), (second_ref, kept_second_ref))
        ):
            for p in range(2):
                total = kept_ref[p * part : (p + 1) * part, :]
                total = total + arrived_ref[p * part : (p + 1) * part, :].astype(F32)
                out_ref[:, p * piece : (p + 1) * piece, q * block : (q + 1) * block] = (
                    total.astype(BF16).reshape(half, piece, block)
                )

    def unpack_rows(in_ref, out_ref):
        for j in range(half):
            for q in range(2):
                at = (q * half + j) * block
                out_ref[:, at : at + block] = in_ref[j, :, q * block : (q + 1) * block]

    def unpack_down(where_ref, in_ref, out_ref):
        for p in range(2):
            which = where_ref[1] if p == 0 else 1 - where_ref[1]
            target = pl.ds(pl.multiple_of(which * piece, piece), piece)
            for j in range(half):
                for q in range(2):
                    at = (q * half + j) * block
                    out_ref[target, at : at + block] = in_ref[
                        j, p * piece : (p + 1) * piece, q * block : (q + 1) * block
                    ]


    frozen_piece = lax.dynamic_slice_in_dim(frozen, group * (block // 2), block // 2, axis=0)
    down_piece = lax.dynamic_slice_in_dim(down.reshape(own, width), group * piece, piece, axis=0)
    up_near = up.reshape(own, out_width)

    up_far = swapped(up_near)

    frozen_near = swapped(after(frozen_piece, up_far))

    cot_at = pair
    up_at = cot_at + 2 * out_width
    id_at = up_at + 2 * out_width
    wide = id_at + LANES

    def pack_small(down_ref, cot_ref, near_ref, far_ref, id_ref, out_ref):
        for j in range(half):
            c = j % 2
            for q in range(2):
                out_ref[j, :, q * block : (q + 1) * block] = down_ref[
                    :, (q * half + j) * block : (q * half + j + 1) * block
                ]
                out_ref[j, :, cot_at + q * out_width : cot_at + (q + 1) * out_width] = cot_ref[
                    (2 * c + q) * piece : (2 * c + q + 1) * piece, :
                ]
            for q, up_ref in enumerate((near_ref, far_ref)):
                out_ref[j, :, up_at + q * out_width : up_at + (q + 1) * out_width] = up_ref[
                    c * piece : (c + 1) * piece, :
                ]
            out_ref[j, :, id_at:] = id_ref[...]

    id_line = jnp.broadcast_to(ids.astype(BF16)[None, :], (piece, LANES))
    small = pl.pallas_call(
        pack_small,
        out_shape=shape(half, piece, wide),
        compiler_params=params,
        cost_estimate=cost(0, 4 * half * piece * wide),
    )(down_piece, cot, up_near, up_far, id_line)
    small = exchange(small)
    down_near = small[:, :, :pair].reshape(half * piece, pair)

    def pack_rows(x_ref, first_ref, second_ref):
        for j in range(half):
            for q, out_ref in enumerate((first_ref, second_ref)):
                out_ref[j, :, :] = x_ref[:, (q * half + j) * block : (q * half + j + 1) * block]

    x_parts = pl.pallas_call(
        pack_rows,
        out_shape=(shape(half, rows, block),) * 2,
        compiler_params=params,
        cost_estimate=cost(0, 4 * rows * width),
    )(x)

    small, frozen_near, x_parts = lax.optimization_barrier((small, frozen_near, x_parts))
    down_near = small[:, :, :pair].reshape(half * piece, pair)

    shared = small[:, :, pair:id_at].reshape(half * piece, 4 * out_width)
    half_ids = small[:, 0, id_at:].reshape(half_rows).astype(F32)
    id_rows = jnp.broadcast_to(half_ids[:, None], (half_rows, LANES))
    id_lines = jnp.broadcast_to(half_ids[None, :], (8, half_rows))

    shared_twin = flipped(shared, 1)

    down_far = swapped(down_near)

    near_cross = other_group(down_near)

    frozen_cross = other_group(frozen_near)

    first_piece = jnp.where(group == 0, frozen_near, frozen_cross)
    last_piece = jnp.where(group == 0, frozen_cross, frozen_near)
    frozen_far = jnp.concatenate([first_piece, last_piece], axis=0)
    frozen_low = jnp.where(my_half == 0, frozen, frozen_far)
    frozen_high = jnp.where(my_half == 0, frozen_far, frozen)

    x_first = exchange(after(x_parts[0], small)).reshape(half_rows, block)

    x_second = exchange(after(x_parts[1], x_first)).reshape(half_rows, block)

    by_row, by_column, half_cot = pl.pallas_call(
        grads_body,
        out_shape=(
            shape(half_rows, columns),
            shape(columns, half_rows),
            shape(half_rows, out_width),
        ),
        in_specs=[smem] + [vmem] * 4,
        out_specs=(vmem, vmem, vmem),
        scratch_shapes=[pltpu.VMEM((columns, out_width), BF16)],
        compiler_params=params,
        cost_estimate=cost(4 * half_rows * columns * out_width, 8 * half_rows * columns),
    )(where, shared, shared_twin, id_rows, id_lines)


    far_cross = other_group(after(down_far, half_cot, frozen_low, frozen_high, x_first))

    maps = (down_near, down_far, near_cross, far_cross)
    result = pl.pallas_call(
        rows_body,
        grid=(half_rows // lines,),
        out_shape=shape(half, rows, pair),
        in_specs=[
            pl.BlockSpec((lines, out_width), lambda i: (i, 0)),
            pl.BlockSpec((lines, columns), lambda i: (i, 0)),
        ]
        + [pl.BlockSpec((block, out_width), lambda i: (0, 0))] * 2
        + [pl.BlockSpec((part, pair), lambda i: (0, 0))] * 4,
        out_specs=pl.BlockSpec((lines // rows, rows, pair), lambda i: (i, 0, 0)),
        compiler_params=params,
        cost_estimate=cost(16000000000, 0),
    )(half_cot, by_row, frozen_low, frozen_high, *maps)


    back = exchange(result)

    sent_first = down_part(1, x_first, BF16)

    arrived_first = swapped(sent_first)

    sent_second = down_part(1, after(x_second, result, arrived_first), BF16)

    arrived_second = swapped(sent_second)

    low = pl.pallas_call(
        low_body,
        grid=(half_rows // lines,),
        out_shape=shape(half_rows // packed, LANES, kind=F32),
        in_specs=[
            smem,
            pl.BlockSpec((lines, block), lambda i: (i, 0)),
            pl.BlockSpec((lines, block), lambda i: (i, 0)),
            pl.BlockSpec((lines, LANES), lambda i: (i, 0)),
        ]
        + [pl.BlockSpec((part, pair), lambda i: (0, 0))] * 4,
        out_specs=pl.BlockSpec((lines // packed, LANES), lambda i: (i, 0)),
        compiler_params=params,
        cost_estimate=cost(2 * half_rows * pair * columns, 2 * half_rows * pair),
    )(where, x_first, after(x_second, sent_second), id_rows, *maps)

    kept_first = down_part(0, after(x_first, low), F32)
    kept_second = down_part(0, after(x_second, low), F32)

    low_sum = low
    for bit in (2, 1):
        low_sum = low_sum + flipped(low_sum, bit)

    joined = lax.optimization_barrier((arrived_first, arrived_second, kept_first, kept_second, low_sum))
    low_sum = joined[4]
    sums = pl.pallas_call(
        add_body,
        out_shape=shape(half, own, pair),
        compiler_params=params,
        cost_estimate=cost(45000000000, 0),
    )(*joined[:4])

    home = exchange(after(sums, back))

    gradient = pl.pallas_call(
        unpack_rows,
        out_shape=shape(rows, width),
        compiler_params=params,
        cost_estimate=cost(0, 4 * rows * width),
    )(back)


    low_all = after(low_sum, sums, gradient)
    low_all = low_all.astype(BF16).reshape(half_rows // lines, lines // packed, packed, rank)
    low_all = low_all.transpose(0, 2, 1, 3).reshape(half_rows, rank)
    plane = half // 2
    planes = n // plane
    level = jnp.bitwise_xor(here // plane, jnp.arange(planes, dtype=jnp.int32))
    adapters = ((level * plane + here % plane) * held)[:, None] + jnp.arange(held, dtype=jnp.int32)
    spread = jnp.where(
        half_ids[:, None] == jnp.repeat(adapters.reshape(-1), rank)[None, :].astype(F32),
        jnp.tile(low_all, (1, planes * held)),
        jnp.zeros((), BF16),
    )
    up_part = (ADAPTER_SCALE * dot(spread, half_cot, ((0,), (0,)))).reshape(planes, own, out_width)
    up_sent = up_part.astype(BF16)

    up_grad = up_part[0]
    for level in range(1, planes):
        up_grad = up_grad + flipped(up_sent[level], level * plane).astype(F32)
    up_grad = up_grad.astype(BF16)

    down_grad = pl.pallas_call(
        unpack_down,
        out_shape=shape(own, width),
        in_specs=[smem, vmem],
        out_specs=vmem,
        compiler_params=params,
        cost_estimate=cost(0, 4 * own * width),
    )(where, after(home, gradient))
    return gradient, down_grad.reshape(held, rank, width), up_grad.reshape(held, rank, out_width)


def on_device(x, cot, ids, frozen, down, up):
    n = lax.axis_size("adapt")
    own = down.shape[0] * down.shape[1]
    fits = (
        lax.axis_size("groups") == 2
        and x.shape[1] // n % (2 * LANES) == 0
        and n == 16
        and down.shape[0] == 2
        and x.shape[0] == 2 * own == LANES
        and cot.shape[1] % LANES == 0
    )
    return (with_kernels if fits else in_xla)(x, cot, ids, frozen, down, up)


def solution(mesh):
    return jax.shard_map(
        on_device,
        mesh=mesh,
        in_specs=(
            P(("groups", "adapt"), None),
            P(("groups", "adapt"), None),
            P(("groups", "adapt")),
            P("adapt", None),
            P("adapt", None, None),
            P("adapt", None, None),
        ),
        out_specs=(
            P(("groups", "adapt"), None),
            P(("groups", "adapt"), None, None),
            P(("groups", "adapt"), None, None),
        ),
        check_vma=False,
    )
```
